256 devices in a mesh: dp: 16 (over y, x_hi, core), tm: 16 (over x_lo, z).
Axes of the slice: x: 4 (x_hi: 2, x_lo: 2; x = x_hi * 2 + x_lo), y: 4, z: 8, core: 2. Of those that a mesh axis runs over, the one named last changes fastest.
Arguments:
- frames_in: bfloat16 [16, 32, 128, 1024], P('dp', 'tm'), may hold values from -8 to 8
- gain: float32 [1024], replicated, may hold values from 0.5 to 1.5
- w_qkv: bfloat16 [1024, 1536], P(('dp', 'tm')), may hold values from -2 to 2
- w_out: bfloat16 [512, 1024], P(None, ('dp', 'tm')), may hold values from -0.25 to 0.25
- out_grad: bfloat16 [16, 32, 128, 1024], P('dp', 'tm'), may hold values from -6 to 6
Outputs:
- result: bfloat16 [16, 32, 128, 1024], P('dp', 'tm')
- grad_in: bfloat16 [16, 32, 128, 1024], P('dp', 'tm')
- grad_qkv: float32 [1024, 1536], P(('dp', 'tm'))
- grad_out: float32 [512, 1024], P(None, ('dp', 'tm'))
- grad_gain: float32 [1024], P(('dp', 'tm'))
The draws below stay inside these ranges and needn't reach their ends.
All inputs are finite; a program needn't handle non-finite values.
Results may differ from the reference program's by a relative error of at most 0.01.
The reference program's roundings to bfloat16 on the way count: a program that leaves them out, or rounds other values in their place, can miss the bound.
Values may be sent and summed in bfloat16 or wider, within the bound.
No kernel may reach another device: no remote copies, remote signals or barrier semaphores. Data moves between devices by JAX's collectives and lax.ppermute only.
A program may use at most 64 MiB of HBM per device.

```python
import jax
import jax.numpy as jnp
from jax import lax

D = 1024
HEADS = 8
DH = 64
PATCH = 128
SAMPLES = 16
FRAMES = 32


def draw_frames_in(key, part):
    key = jax.random.fold_in(key, 11)
    key_noise = jax.random.fold_in(key, 0)
    noise = jax.random.normal(key_noise, (SAMPLES, FRAMES, PATCH, D), jnp.float32)
    values = noise
    return jnp.clip(values, -8.0, 8.0).astype(jnp.bfloat16)


def draw_w_qkv(key, part):
    key = jax.random.fold_in(key, 12)
    key_noise = jax.random.fold_in(key, 0)
    width_heads = HEADS * DH
    noise = jax.random.normal(key_noise, (D, 3 * width_heads), jnp.float32) * D ** (-0.5)
    values = noise
    return jnp.clip(values, -2.0, 2.0).astype(jnp.bfloat16)


def levels(rng, shape, shards, smallest, largest):
    factor_of, own = 1.0, jax.random.fold_in(rng, 6)
    for position, blocks in shards:
        steps = jnp.exp(jax.random.uniform(jax.random.fold_in(own, position), (blocks,), jnp.float32, smallest / len(shards), largest / len(shards)))
        factor_of = factor_of * jnp.repeat(steps, shape[position] // blocks).reshape([-1 if axis == position else 1 for axis in range(len(shape))])
    return factor_of


def normal_values(stream_key, shape, scale, reach, pieces=(), held_as=jnp.bfloat16):
    factor_of = levels(stream_key, shape, pieces, -0.22, 0.18) if pieces else 1.0
    values = jax.random.normal(stream_key, shape, jnp.float32) * scale * factor_of
    return jnp.minimum(jnp.maximum(values, -reach), reach).astype(held_as)


def setup_inputs(seed: int = 0) -> dict:
    streams_of = jax.random.split(jax.random.key(seed), 6)
    return {
        "frames_in": draw_frames_in(jax.random.fold_in(streams_of[5], 71), 0),
        "gain": jnp.clip(1.0 + 0.1 * jax.random.normal(streams_of[1], (D,), jnp.float32), 0.5, 1.5),
        "w_qkv": draw_w_qkv(jax.random.fold_in(streams_of[5], 71), 0),
        "w_out": normal_values(streams_of[3], (HEADS * DH, D), (HEADS * DH) ** -0.5, 0.25, ((1, 256),)),
        "out_grad": normal_values(streams_of[4], (SAMPLES, FRAMES, PATCH, D), 1.0, 6.0, ((0, 16), (1, 16))),
    }


norm_eps = 1e-05

def layer_stats(features, gain):
    wide = features.astype(jnp.float32)
    mean_val = lax.optimization_barrier(jnp.mean(wide, axis=-1, keepdims=True))
    centred = wide - mean_val
    inv_std = lax.rsqrt(lax.optimization_barrier(jnp.mean(centred * centred, axis=-1, keepdims=True)) + norm_eps)
    normal_x = centred * inv_std
    normed = (normal_x * gain).astype(jnp.bfloat16)
    return (wide, normal_x, inv_std, normed)

def split_heads(packed):
    frame_count, patch_count = (packed.shape[0], packed.shape[1])
    parts = packed.reshape(frame_count, patch_count, 3, HEADS, DH).transpose(2, 1, 3, 0, 4)
    return (parts[0], parts[1], parts[2])

def merge_heads(per_head):
    patch_count, head_count, frame_count, head_dim = per_head.shape
    return per_head.transpose(2, 0, 1, 3).reshape(frame_count, patch_count, head_count * head_dim)

def attend(packed):
    query, keys, values = split_heads(packed)
    scores = jnp.einsum('phfd,phgd->phfg', query.astype(jnp.float32), keys.astype(jnp.float32)) * DH ** (-0.5)
    top_val = lax.optimization_barrier(jnp.max(scores, axis=-1, keepdims=True))
    expo = jnp.exp(scores - top_val)
    prob = expo / lax.optimization_barrier(jnp.sum(expo, axis=-1, keepdims=True))
    prob_low = prob.astype(jnp.bfloat16)
    mixed = jnp.einsum('phfg,phgd->phfd', prob_low.astype(jnp.float32), values.astype(jnp.float32)).astype(jnp.bfloat16)
    return (merge_heads(mixed), prob)

def attend_back(packed, prob, d_mixed):
    query, keys, values = split_heads(packed)
    frame_count, patch_count = (d_mixed.shape[0], d_mixed.shape[1])
    d_heads = d_mixed.reshape(frame_count, patch_count, HEADS, DH).transpose(1, 2, 0, 3).astype(jnp.float32)
    prob_low = prob.astype(jnp.bfloat16).astype(jnp.float32)
    d_prob = jnp.einsum('phfd,phgd->phfg', d_heads, values.astype(jnp.float32))
    d_values = jnp.einsum('phfg,phfd->phgd', prob_low, d_heads).astype(jnp.bfloat16)
    inner = lax.optimization_barrier(jnp.sum(d_prob * prob, axis=-1, keepdims=True))
    d_scores = (prob * (d_prob - inner) * DH ** (-0.5)).astype(jnp.bfloat16).astype(jnp.float32)
    d_query = jnp.einsum('phfg,phgd->phfd', d_scores, keys.astype(jnp.float32)).astype(jnp.bfloat16)
    d_keys = jnp.einsum('phfg,phfd->phgd', d_scores, query.astype(jnp.float32)).astype(jnp.bfloat16)
    stacked = jnp.stack([d_query, d_keys, d_values])
    return stacked.transpose(3, 1, 0, 2, 4).reshape(frame_count, patch_count, 3 * HEADS * DH)

def reference(frames_in, gain, w_qkv, w_out, out_grad):

    def one_sample(pair):
        features, cotangent = pair
        frame_count, patch_count, width = features.shape
        row_count = frame_count * patch_count
        wide, normal_x, inv_std, normed = layer_stats(features, gain)
        normed_rows = normed.reshape(row_count, width)
        packed = jnp.dot(normed_rows, w_qkv, preferred_element_type=jnp.float32).astype(jnp.bfloat16)
        packed = packed.reshape(frame_count, patch_count, 3 * HEADS * DH)
        mixed, prob = attend(packed)
        mixed_rows = mixed.reshape(row_count, HEADS * DH)
        result = (wide.reshape(row_count, width) + jnp.dot(mixed_rows, w_out, preferred_element_type=jnp.float32)).astype(jnp.bfloat16)
        grad_rows = cotangent.reshape(row_count, width)
        grad_out = jnp.dot(mixed_rows.T, grad_rows, preferred_element_type=jnp.float32)
        d_mixed = jnp.dot(grad_rows, w_out.T, preferred_element_type=jnp.float32).astype(jnp.bfloat16)
        d_packed = attend_back(packed, prob, d_mixed.reshape(frame_count, patch_count, HEADS * DH))
        d_packed = d_packed.reshape(row_count, 3 * HEADS * DH)
        grad_qkv = jnp.dot(normed_rows.T, d_packed, preferred_element_type=jnp.float32)
        d_normed = jnp.dot(d_packed, w_qkv.T, preferred_element_type=jnp.float32).astype(jnp.bfloat16)
        d_normed = d_normed.reshape(features.shape).astype(jnp.float32)
        grad_gain = lax.optimization_barrier(jnp.sum(d_normed * normal_x, axis=(0, 1)))
        scaled = d_normed * gain
        d_input = inv_std * (scaled - lax.optimization_barrier(jnp.mean(scaled, axis=-1, keepdims=True)) - normal_x * lax.optimization_barrier(jnp.mean(scaled * normal_x, axis=-1, keepdims=True)))
        grad_in = (cotangent.astype(jnp.float32) + d_input).astype(jnp.bfloat16)
        return (result.reshape(features.shape), grad_in, grad_qkv, grad_out, grad_gain)
    outputs = lax.map(one_sample, (frames_in, out_grad))
    return (outputs[0], outputs[1], lax.optimization_barrier(jnp.sum(outputs[2], axis=0)), lax.optimization_barrier(jnp.sum(outputs[3], axis=0)), lax.optimization_barrier(jnp.sum(outputs[4], axis=0)))
```

```python
import functools

import jax
import jax.numpy as jnp
from jax import lax
from jax.experimental import pallas as pl
from jax.experimental.pallas import tpu as pltpu
from jax.sharding import Mesh, PartitionSpec as P

DP = ("y", "xh", "core")
TM = ("xl", "z")
GROUP = ("y", "xh")

D = 1024
DH = 64
HALF = 256
norm_eps = 1e-05
f32 = jnp.float32
bf16 = jnp.bfloat16

NN = (((1,), (0,)), ((), ()))
NT = (((1,), (1,)), ((), ()))
TN = (((0,), (0,)), ((), ()))


def mm(a, b, dims):
    return lax.dot_general(a, b, dims, preferred_element_type=f32)


def layer_stats(features):
    wide = features.astype(f32)
    centred = wide - jnp.mean(wide, axis=-1, keepdims=True)
    inv_std = lax.rsqrt(jnp.mean(centred * centred, axis=-1, keepdims=True) + norm_eps)
    return centred * inv_std, inv_std


def attention_kernel(patches, x_ref, og_ref, gain_ref, w_ref, normed_ref, mixed_ref, dpacked_ref):
    rows = x_ref.shape[1]
    row_patch = lax.broadcasted_iota(jnp.int32, (rows, rows), 0) % patches
    col_patch = lax.broadcasted_iota(jnp.int32, (rows, rows), 1) % patches
    same = row_patch == col_patch
    low_half = lax.broadcasted_iota(jnp.int32, (rows, 2 * DH), 1) < DH
    zero = jnp.zeros((rows, 2 * DH), bf16)
    for s in range(2):
        normal_x, _ = layer_stats(x_ref[s])
        normed = (normal_x * gain_ref[...]).astype(bf16)
        normed_ref[s] = normed
        packed = mm(normed, w_ref[:, : 3 * HALF], NN).astype(bf16)
        d_mixed = mm(og_ref[s], w_ref[:, 3 * HALF :], NN).astype(bf16)
        for pair in range(HALF // (2 * DH)):
            lo = pair * 2 * DH
            query = packed[:, lo : lo + 2 * DH]
            keys = packed[:, HALF + lo : HALF + lo + 2 * DH]
            values = packed[:, 2 * HALF + lo : 2 * HALF + lo + 2 * DH]
            d_heads = d_mixed[:, lo : lo + 2 * DH]
            parts = []
            for head in range(2):
                own = low_half if head == 0 else jnp.logical_not(low_half)
                scores = mm(jnp.where(own, query, zero), keys, NT) * DH ** (-0.5)
                scores = jnp.where(same, scores, -1e30)
                expo = jnp.exp(scores - jnp.max(scores, axis=-1, keepdims=True))
                prob = expo / jnp.sum(expo, axis=-1, keepdims=True)
                prob_low = prob.astype(bf16)
                mixed = mm(prob_low, values, NN)
                d_prob = mm(jnp.where(own, d_heads, zero), values, NT)
                d_values = mm(prob_low, d_heads, TN)
                inner = jnp.sum(d_prob * prob, axis=-1, keepdims=True)
                d_scores = (prob * (d_prob - inner) * DH ** (-0.5)).astype(bf16)
                d_query = mm(d_scores, keys, NN)
                d_keys = mm(d_scores, query, TN)
                parts.append((mixed, d_query, d_keys, d_values))
            mixed, d_query, d_keys, d_values = (
                jnp.where(low_half, a, b).astype(bf16) for a, b in zip(*parts)
            )
            mixed_ref[s, :, lo : lo + 2 * DH] = mixed
            dpacked_ref[s, :, lo : lo + 2 * DH] = d_query
            dpacked_ref[s, :, HALF + lo : HALF + lo + 2 * DH] = d_keys
            dpacked_ref[s, :, 2 * HALF + lo : 2 * HALF + lo + 2 * DH] = d_values


def gradient_kernel(normed_ref, og_ref, dpacked_ref, mixed_ref, g_ref):
    g_ref[:, : 3 * HALF] = mm(normed_ref[...], dpacked_ref[...], TN).astype(bf16)
    g_ref[:, 3 * HALF :] = mm(og_ref[...], mixed_ref[...], TN).astype(bf16)


def input_kernel(x_ref, og_ref, gain_ref, dp_mine_ref, dp_other_ref, w_mine_ref, w_other_ref, out_ref):
    d_normed = mm(dp_mine_ref[...], w_mine_ref[:, : 3 * HALF], NT)
    d_normed = d_normed + mm(dp_other_ref[...], w_other_ref[:, : 3 * HALF], NT)
    d_normed = d_normed.astype(bf16).astype(f32)
    normal_x, inv_std = layer_stats(x_ref[...])
    scaled = d_normed * gain_ref[...]
    d_input = inv_std * (
        scaled
        - jnp.mean(scaled, axis=-1, keepdims=True)
        - normal_x * jnp.mean(scaled * normal_x, axis=-1, keepdims=True)
    )
    out_ref[...] = (og_ref[...].astype(f32) + d_input).astype(bf16)


def result_kernel(x_ref, mixed_ref, w_mine_ref, w_other_ref, out_ref):
    projected = mm(mixed_ref[:, :HALF], w_mine_ref[...], NT)
    projected = projected + mm(mixed_ref[:, HALF:], w_other_ref[...], NT)
    out_ref[...] = (x_ref[...].astype(f32) + projected).astype(bf16)


def vmem_params():
    return pltpu.CompilerParams(vmem_limit_bytes=48 * 1024 * 1024)


def exchange(value):
    return lax.ppermute(value, "core", [(0, 1), (1, 0)])


def swap(value, axes):
    return lax.all_to_all(value, axes, split_axis=0, concat_axis=0, tiled=True)


def body(frames_in, gain, w_qkv, w_out, out_grad):
    _, frames, patch_count, width = frames_in.shape
    tm = 16
    group = 8
    patches = patch_count // tm
    per_peer = frames * patches
    rows = tm * per_peer
    shard = w_qkv.shape[0]
    core = lax.axis_index("core")
    gain_row = gain.reshape(1, width)

    def by_patch(value):
        value = value.reshape(frames, tm, patches, width).transpose(1, 0, 2, 3)
        return value.reshape(tm, per_peer, width)

    w_parts = jnp.concatenate([w_qkv.reshape(shard, 3, 2, HALF), w_out.T.reshape(shard, 1, 2, HALF)], axis=1)
    w_parts = w_parts.transpose(2, 0, 1, 3).reshape(1, 2 * shard, 4 * HALF)
    w_parts = jnp.broadcast_to(w_parts, (tm, 2 * shard, 4 * HALF))
    sent = jnp.concatenate([by_patch(frames_in), by_patch(out_grad), w_parts], axis=1)
    got = swap(sent.reshape(-1, width), TM).reshape(tm, 2 * per_peer + 2 * shard, width)
    x_own = got[:, :per_peer].reshape(rows, width)
    og_own = got[:, per_peer : 2 * per_peer].reshape(rows, width)
    w_got = got[:, 2 * per_peer :].reshape(tm, 2, shard, width)

    w_keep = lax.dynamic_index_in_dim(w_got, core, 1, keepdims=False).reshape(tm * shard, width)
    w_send = lax.dynamic_index_in_dim(w_got, 1 - core, 1, keepdims=False).reshape(tm * shard, width)
    w_recv = exchange(w_send)
    first = core == 0
    w_block = jnp.concatenate(
        [jnp.where(first, w_keep, w_recv), jnp.where(first, w_recv, w_keep)], axis=0
    )
    w_mine = swap(jnp.broadcast_to(w_block[None], (group,) + w_block.shape).reshape(width, width), GROUP)
    w_other = exchange(w_mine)

    x_both = jnp.stack([x_own, exchange(x_own)])
    og_both = jnp.stack([og_own, exchange(og_own)])

    normed, mixed, d_packed = pl.pallas_call(
        functools.partial(attention_kernel, patches),
        out_shape=(
            jax.ShapeDtypeStruct((2, rows, width), bf16),
            jax.ShapeDtypeStruct((2, rows, HALF), bf16),
            jax.ShapeDtypeStruct((2, rows, 3 * HALF), bf16),
        ),
        compiler_params=vmem_params(),
        cost_estimate=pl.CostEstimate(flops=3 * 10**9, bytes_accessed=8 * 2**20, transcendentals=2**19),
        name="attention",
    )(x_both, og_both, gain_row, w_mine)

    grads = pl.pallas_call(
        gradient_kernel,
        out_shape=jax.ShapeDtypeStruct((width, 4 * HALF), bf16),
        compiler_params=vmem_params(),
        cost_estimate=pl.CostEstimate(flops=10**9, bytes_accessed=6 * 2**20, transcendentals=0),
        name="gradients",
    )(
        normed.reshape(2 * rows, width),
        og_both.reshape(2 * rows, width),
        d_packed.reshape(2 * rows, 3 * HALF),
        mixed.reshape(2 * rows, HALF),
    )
    dp_other = exchange(d_packed[1])
    mixed_other = exchange(mixed[1])

    grads = swap(grads, GROUP).reshape(group, 2, tm, shard, width)
    grads = jnp.sum(grads.astype(f32), axis=0)
    grads = grads.transpose(1, 0, 2, 3).reshape(tm, 2 * shard, width).astype(bf16)

    grad_in = pl.pallas_call(
        input_kernel,
        out_shape=jax.ShapeDtypeStruct((rows, width), bf16),
        compiler_params=vmem_params(),
        cost_estimate=pl.CostEstimate(flops=10**9, bytes_accessed=6 * 2**20, transcendentals=0),
        name="input_gradient",
    )(x_own, og_own, gain_row, d_packed[0], dp_other, w_mine, w_other)

    mixed_own = jnp.concatenate([mixed[0], mixed_other], axis=1)
    mixed_own = mixed_own.reshape(tm, frames, patches, 2 * HALF).transpose(0, 2, 1, 3)
    mixed_own = mixed_own.reshape(tm, patches, frames * 2 * HALF)
    sent = jnp.concatenate([grad_in.reshape(tm, per_peer, width), mixed_own, grads], axis=1)
    got = swap(sent.reshape(-1, width), TM).reshape(sent.shape)
    grad_in = got[:, :per_peer].reshape(tm, frames, patches, width).transpose(1, 0, 2, 3)
    grad_in = grad_in.reshape(frames_in.shape)
    mixed_home = got[:, per_peer : per_peer + patches].reshape(tm, patches, frames, 2 * HALF)
    mixed_home = mixed_home.transpose(2, 0, 1, 3).reshape(rows, 2 * HALF)
    result = pl.pallas_call(
        result_kernel,
        out_shape=jax.ShapeDtypeStruct((rows, width), bf16),
        compiler_params=vmem_params(),
        cost_estimate=pl.CostEstimate(flops=3 * 10**8, bytes_accessed=3 * 2**20, transcendentals=0),
        name="result",
    )(frames_in.reshape(rows, width), mixed_home, w_mine[:, 3 * HALF :], w_other[:, 3 * HALF :])

    total = jnp.sum(got[:, per_peer + patches :].astype(f32), axis=0).reshape(2, shard, width)
    keep = lax.dynamic_index_in_dim(total, core, 0, keepdims=False)
    recv = exchange(lax.dynamic_index_in_dim(total, 1 - core, 0, keepdims=False))
    low = jnp.where(first, keep, recv).reshape(shard, 4, 1, HALF)
    high = jnp.where(first, recv, keep).reshape(shard, 4, 1, HALF)
    whole = jnp.concatenate([low, high], axis=2)
    grad_qkv = whole[:, :3].reshape(shard, 6 * HALF)
    grad_out = whole[:, 3].reshape(shard, 2 * HALF).T
    own_row = lax.axis_index(DP + TM) * shard
    grad_gain = jnp.sum(w_qkv.astype(f32) * grad_qkv, axis=1) / lax.dynamic_slice_in_dim(gain, own_row, shard)
    return (result.reshape(frames_in.shape), grad_in, grad_qkv, grad_out, grad_gain)


def solution(mesh):
    fine = Mesh(mesh.devices.reshape(4, 2, 2, 2, 8), DP + TM)
    in_specs = (
        P(DP, TM, None, None),
        P(),
        P(DP + TM, None),
        P(None, DP + TM),
        P(DP, TM, None, None),
    )
    out_specs = (
        P(DP, TM, None, None),
        P(DP, TM, None, None),
        P(DP + TM, None),
        P(None, DP + TM),
        P(DP + TM),
    )
    return jax.shard_map(body, mesh=fine, in_specs=in_specs, out_specs=out_specs, check_vma=False)
```

```python
import functools

import jax
import jax.numpy as jnp
from jax import lax
from jax.experimental import pallas as pl
from jax.experimental.pallas import tpu as pltpu
from jax.sharding import Mesh, PartitionSpec as P

DP = ("y", "xh", "core")
TM = ("xl", "z")
Y_SIZE, XH_SIZE, TM_SIZE = 4, 2, 16

D = 1024
DH = 64
HALF = 256
norm_eps = 1e-05
f32 = jnp.float32
bf16 = jnp.bfloat16

NN = (((1,), (0,)), ((), ()))
NT = (((1,), (1,)), ((), ()))
TN = (((0,), (0,)), ((), ()))

SMEM = pl.BlockSpec(memory_space=pltpu.SMEM)
VMEM = pl.BlockSpec(memory_space=pltpu.VMEM)
HBM = pl.BlockSpec(memory_space=pl.ANY)


def mm(a, b, dims):
    return lax.dot_general(a, b, dims, preferred_element_type=f32)


def layer_stats(features):
    wide = features.astype(f32)
    centred = wide - jnp.mean(wide, axis=-1, keepdims=True)
    inv_std = lax.rsqrt(jnp.mean(centred * centred, axis=-1, keepdims=True) + norm_eps)
    return centred * inv_std, inv_std


def attend(pair, same, low_half, packed, d_mixed):
    lo = pair * 2 * DH
    query = packed[:, lo : lo + 2 * DH]
    keys = packed[:, HALF + lo : HALF + lo + 2 * DH]
    values = packed[:, 2 * HALF + lo : 2 * HALF + lo + 2 * DH]
    d_heads = d_mixed[:, lo : lo + 2 * DH]
    zero = jnp.zeros_like(query)
    parts = []
    for own in (low_half, jnp.logical_not(low_half)):
        scores = mm(jnp.where(own, query * DH ** (-0.5), zero), keys, NT)
        scores = jnp.where(same, scores, -1e30)
        expo = jnp.exp(scores - jnp.max(scores, axis=-1, keepdims=True))
        prob = expo * (1.0 / jnp.sum(expo, axis=-1, keepdims=True))
        prob_low = prob.astype(bf16)
        mixed = mm(prob_low, values, NN)
        d_prob = mm(jnp.where(own, d_heads, zero), values, NT)
        d_values = mm(prob_low, d_heads, TN)
        inner = jnp.sum(d_prob * prob, axis=-1, keepdims=True)
        d_scores = (prob * (d_prob - inner)).astype(bf16)
        d_query = mm(d_scores, keys, NN) * DH ** (-0.5)
        d_keys = mm(d_scores, query, TN) * DH ** (-0.5)
        parts.append((mixed, d_query, d_keys, d_values))
    return [jnp.where(low_half, a, b).astype(bf16) for a, b in zip(*parts)]


def pack_weights_kernel(w_qkv_ref, w_out_ref, out_ref):
    qkv, out = w_qkv_ref[...].astype(f32), w_out_ref[...].astype(f32)
    halves = []
    for half in range(2):
        parts = [qkv[:, (2 * part + half) * HALF : (2 * part + half + 1) * HALF] for part in range(3)]
        halves.append(jnp.concatenate(parts + [out[:, half * HALF : (half + 1) * HALF]], axis=1))
    both = jnp.concatenate(halves, axis=0)
    out_ref[...] = jnp.broadcast_to(both[None], out_ref.shape).astype(bf16)


def fetch(pairs, sems, first=0):
    copies = [pltpu.make_async_copy(src, dst, sems.at[first + i]) for i, (src, dst) in enumerate(pairs)]
    for copy in copies:
        copy.start()
    return copies


def wait_all(copies):
    for copy in copies:
        copy.wait()


def sample(patches, got, gain_ref, weights, normed, mixed, dpacked, before_weights, after_weights):
    rows = normed.shape[0]
    row_patch = lax.broadcasted_iota(jnp.int32, (rows, rows), 0) % patches
    col_patch = lax.broadcasted_iota(jnp.int32, (rows, rows), 1) % patches
    same = row_patch == col_patch
    low_half = lax.broadcasted_iota(jnp.int32, (rows, 2 * DH), 1) < DH
    per_peer = got.shape[1] // 2
    normal_x, _ = layer_stats(got[:, :per_peer, :].reshape(rows, D))
    normed[...] = (normal_x * gain_ref[...]).astype(bf16)
    before_weights()
    packed = mm(normed[...], weights[:, : 3 * HALF], NN).astype(bf16)
    d_mixed = mm(got[:, per_peer:, :].reshape(rows, D), weights[:, 3 * HALF :], NN).astype(bf16)
    after_weights()
    for pair in range(HALF // (2 * DH)):
        lo = pair * 2 * DH
        outs = attend(pair, same, low_half, packed, d_mixed)
        mixed[:, lo : lo + 2 * DH] = outs[0]
        for part in range(3):
            at = part * HALF + lo
            dpacked[:, at : at + 2 * DH] = outs[1 + part]


def own_kernel(patches, place_ref, got_ref, gain_ref, *refs):
    pieces, (w_out_ref, normed_ref, mixed_ref, dpacked_ref) = refs[:8], refs[8:12]
    got, weights, normed, mixed, dpacked, sems = refs[12:]
    (copy_got,) = fetch([(got_ref, got)], sems)
    block = pieces[0].shape[0]
    starts = [pl.multiple_of(place_ref[i] * block, block) for i in range(8)]
    copies = fetch([(p, weights.at[pl.ds(at, block), :]) for p, at in zip(pieces, starts)], sems, 1)
    results = []

    def before_weights():
        results.extend(fetch([(normed, normed_ref)], sems, 9))
        wait_all(copies)

    def after_weights():
        results.extend(fetch([(weights, w_out_ref)], sems, 10))

    copy_got.wait()
    sample(patches, got, gain_ref, weights, normed, mixed, dpacked, before_weights, after_weights)
    results.extend(fetch([(mixed, mixed_ref), (dpacked, dpacked_ref)], sems, 11))
    wait_all(results)


def other_kernel(patches, place_ref, got_own_ref, got_ref, gain_ref, w_ref, *refs):
    (normed_ref, mixed_ref, dpacked_ref, mixed_out_ref, dpacked_out_ref), outs = refs[:5], refs[5:13]
    got, weights, og, normed, mixed, dpacked, grads, own, peers, sems = refs[13:]
    per_peer = og.shape[2]
    copies = fetch(
        [
            (got_ref, got),
            (w_ref, weights),
            (got_own_ref.at[:, per_peer:, :], og.at[0]),
            (normed_ref, normed.at[0]),
            (mixed_ref, mixed.at[0]),
            (dpacked_ref, dpacked.at[0]),
        ],
        sems,
    )

    def before_weights():
        wait_all(copies[1:])

    def after_weights():
        og[1] = got[:, per_peer:, :]

    copies[0].wait()
    sample(patches, got, gain_ref, weights, normed.at[1], mixed.at[1], dpacked.at[1], before_weights, after_weights)
    results = fetch([(mixed.at[1], mixed_out_ref), (dpacked.at[1], dpacked_out_ref)], sems)
    rows = normed.shape[1]
    block = own.shape[1]
    pair_rows = 2 * block
    all_dpacked = dpacked[...].reshape(2 * rows, 3 * HALF)
    all_mixed = mixed[...].reshape(2 * rows, HALF)
    for step in (1, 2, 3, 0):
        columns = pl.ds(pl.multiple_of(place_ref[8 + step] * pair_rows, pair_rows), pair_rows)
        grads[:, : 3 * HALF] = mm(normed[:, :, columns].reshape(2 * rows, pair_rows), all_dpacked, TN)
        grads[:, 3 * HALF :] = mm(og[:, :, :, columns].reshape(2 * rows, pair_rows), all_mixed, TN)
        for side in range(XH_SIZE):
            start = pl.multiple_of(place_ref[12 + side] * block, block)
            slot = own.at[side] if step == 0 else peers.at[side * (Y_SIZE - 1) + step - 1]
            slot[...] = grads[pl.ds(start, block), :].astype(slot.dtype)
            results += fetch([(slot, outs[side * Y_SIZE + step])], sems, 4 + len(results))
    wait_all(results)


def input_kernel(*refs):
    sources, (gain_ref, out_ref), scratch = refs[:7], refs[7:9], refs[9:]
    got, dp_mine, dp_other, mixed, mixed_other, w_mine, w_other, sems = scratch
    copies = fetch(
        [
            (sources[0], got),
            (sources[1], dp_mine),
            (sources[2], dp_other),
            (sources[3], mixed),
            (sources[4], mixed_other),
            (sources[5].at[:, : 3 * HALF], w_mine),
            (sources[6].at[:, : 3 * HALF], w_other),
        ],
        sems,
    )
    rows = dp_other.shape[0]
    per_peer = got.shape[1] // 2
    copies[0].wait()
    normal_x, inv_std = layer_stats(got[:, :per_peer, :].reshape(rows, D))
    wait_all(copies[1:])
    d_normed = mm(dp_mine[...], w_mine[...], NT) + mm(dp_other[...], w_other[...], NT)
    d_normed = d_normed.astype(bf16).astype(f32)
    scaled = d_normed * gain_ref[...]
    d_input = inv_std * (
        scaled
        - jnp.mean(scaled, axis=-1, keepdims=True)
        - normal_x * jnp.mean(scaled * normal_x, axis=-1, keepdims=True)
    )
    og = got[:, per_peer:, :].reshape(rows, D).astype(f32)
    grad_in = (og + d_input).astype(bf16)
    peers = got.shape[0]
    out_ref[:, :per_peer, :] = grad_in[:, : D // 2].reshape(peers, per_peer, D // 2)
    out_ref[:, per_peer : 2 * per_peer, :] = grad_in[:, D // 2 :].reshape(peers, per_peer, D // 2)
    out_ref[:, 2 * per_peer :, :HALF] = mixed[...].reshape(peers, per_peer, HALF)
    out_ref[:, 2 * per_peer :, HALF:] = mixed_other[...].reshape(peers, per_peer, HALF)


def sum_kernel(own_ref, a_ref, b_ref, c_ref, across_ref, out_ref):
    total = own_ref[...] + a_ref[...].astype(f32) + b_ref[...].astype(f32) + c_ref[...].astype(f32)
    total = total + across_ref[...].astype(f32)
    shard = 4
    low, high = (total.reshape(2, -1, 2 * shard, D)[core] for core in range(2))
    top = lax.broadcasted_iota(jnp.int32, low.shape, 1) < shard
    even = jnp.where(top, low, pltpu.roll(high, shard, 1))
    odd = jnp.where(top, pltpu.roll(low, shard, 1), high)
    out_ref[...] = jnp.stack([even, odd], axis=1).reshape(out_ref.shape).astype(bf16)


def home_kernel(got_ref, x_ref, w_mine_ref, w_other_ref, result_ref, grad_ref, got, x, w_mine, w_other, result, grad, sems):
    output = slice(3 * HALF, 4 * HALF)
    wait_all(
        fetch(
            [(got_ref, got), (x_ref, x), (w_mine_ref.at[:, output], w_mine), (w_other_ref.at[:, output], w_other)],
            sems,
        )
    )
    peers, _, width = got.shape
    frames, count, _ = x.shape
    patches = count // peers
    per_peer = frames * patches

    def by_frame(part):
        wide = got[:, part * per_peer : (part + 1) * per_peer, :].astype(f32)
        wide = wide.reshape(peers, frames, patches, width)
        return [wide[:, f].reshape(count, width).astype(bf16) for f in range(frames)]

    low, high, heads = by_frame(0), by_frame(1), by_frame(2)
    for f in range(frames):
        grad[f, :, :width] = low[f]
        grad[f, :, width:] = high[f]
    results = fetch([(grad, grad_ref)], sems)
    for f in range(frames):
        projected = mm(heads[f][:, :HALF], w_mine[...], NT) + mm(heads[f][:, HALF:], w_other[...], NT)
        result[f] = (x[f].astype(f32) + projected).astype(bf16)
    wait_all(results + fetch([(result, result_ref)], sems, 1))


def vmem_params():
    return pltpu.CompilerParams(vmem_limit_bytes=60 * 1024 * 1024)


def exchange(value):
    return lax.ppermute(value, "core", [(0, 1), (1, 0)])


def swap(value, axes):
    return lax.all_to_all(value, axes, split_axis=0, concat_axis=0, tiled=True)


def along_y(value, step):
    return lax.ppermute(value, "y", [(i, (i + step) % Y_SIZE) for i in range(Y_SIZE)])


def across_x(value):
    return lax.ppermute(value, "xh", [(0, 1), (1, 0)])


def body(frames_in, gain, w_qkv, w_out, out_grad):
    _, frames, patch_count, width = frames_in.shape
    tm = TM_SIZE
    patches = patch_count // tm
    per_peer = frames * patches
    rows = tm * per_peer
    shard = w_qkv.shape[0]
    core = lax.axis_index("core")
    first = core == 0
    y, xh = lax.axis_index("y"), lax.axis_index("xh")
    gain_row = gain.reshape(1, width)

    def by_patch(value):
        value = value.reshape(frames, tm, patches, width).transpose(1, 0, 2, 3)
        return value.reshape(tm, per_peer, width)

    w_parts = pl.pallas_call(
        pack_weights_kernel,
        out_shape=jax.ShapeDtypeStruct((tm, 2 * shard, width), bf16),
        in_specs=[VMEM] * 2,
        compiler_params=vmem_params(),
        cost_estimate=pl.CostEstimate(flops=0, bytes_accessed=2**18, transcendentals=0),
        name="pack_weights",
    )(w_qkv, w_out.T)
    w_got = swap(w_parts.reshape(-1, width), TM).reshape(tm, 2, shard, width)

    w_keep = lax.dynamic_index_in_dim(w_got, core, 1, keepdims=False).reshape(tm * shard, width)
    w_send = lax.dynamic_index_in_dim(w_got, 1 - core, 1, keepdims=False).reshape(tm * shard, width)
    w_recv = exchange(w_send)
    w_block = jnp.concatenate(
        [jnp.where(first, w_keep, w_recv), jnp.where(first, w_recv, w_keep)], axis=0
    )
    block = w_block.shape[0]

    sent = jnp.concatenate([by_patch(frames_in), by_patch(out_grad)], axis=1)
    sent, w_block = lax.optimization_barrier((sent, w_block))
    got = swap(sent.reshape(-1, width), TM).reshape(tm, 2 * per_peer, width)

    pieces, places = [], []
    for side, part in enumerate((w_block, across_x(w_block))):
        for step in range(Y_SIZE):
            pieces.append(part if step == 0 else along_y(part, step))
            places.append(((y + Y_SIZE - step) % Y_SIZE) * 2 + (xh ^ side))
    places += [(y + step) % Y_SIZE for step in range(Y_SIZE)] + [xh, xh ^ 1]
    place = jnp.stack(places).astype(jnp.int32)
    got, *pieces = lax.optimization_barrier((got, *pieces))
    got_other = exchange(got)

    shape = jax.ShapeDtypeStruct
    sample_shapes = (shape((rows, HALF), bf16), shape((rows, 3 * HALF), bf16))
    w_mine, normed, mixed, d_packed = pl.pallas_call(
        functools.partial(own_kernel, patches),
        in_specs=[SMEM, HBM, VMEM] + [HBM] * 8,
        out_specs=(HBM,) * 4,
        out_shape=(shape((width, width), bf16), shape((rows, width), bf16)) + sample_shapes,
        scratch_shapes=[
            pltpu.VMEM(got.shape, bf16),
            pltpu.VMEM((width, width), bf16),
            pltpu.VMEM((rows, width), bf16),
            pltpu.VMEM((rows, HALF), bf16),
            pltpu.VMEM((rows, 3 * HALF), bf16),
            pltpu.SemaphoreType.DMA((13,)),
        ],
        compiler_params=vmem_params(),
        cost_estimate=pl.CostEstimate(flops=2 * 10**9, bytes_accessed=6 * 2**20, transcendentals=2**18),
        name="own_sample",
    )(place, got, gain_row, *pieces)
    w_mine, got_other = lax.optimization_barrier((w_mine, got_other))
    w_other = exchange(w_mine)

    half_shape, own_shape = shape((block, width), bf16), shape((block, width), f32)
    mixed_2, d_packed_2, *grad_pieces = pl.pallas_call(
        functools.partial(other_kernel, patches),
        in_specs=[SMEM, HBM, HBM, VMEM] + [HBM] * 4,
        out_specs=(HBM,) * 10,
        out_shape=sample_shapes + ((own_shape,) + (half_shape,) * (Y_SIZE - 1)) * 2,
        scratch_shapes=[
            pltpu.VMEM(got.shape, bf16),
            pltpu.VMEM((width, width), bf16),
            pltpu.VMEM((2, tm, per_peer, width), bf16),
            pltpu.VMEM((2, rows, width), bf16),
            pltpu.VMEM((2, rows, HALF), bf16),
            pltpu.VMEM((2, rows, 3 * HALF), bf16),
            pltpu.VMEM((2 * block, width), f32),
            pltpu.VMEM((2, block, width), f32),
            pltpu.VMEM((6, block, width), bf16),
            pltpu.SemaphoreType.DMA((16,)),
        ],
        compiler_params=vmem_params(),
        cost_estimate=pl.CostEstimate(flops=3 * 10**9, bytes_accessed=10 * 2**20, transcendentals=2**18),
        name="other_sample",
    )(place, got, got_other, gain_row, w_mine, normed, mixed, d_packed)
    dp_other = exchange(d_packed_2)
    mixed_other = exchange(mixed_2)

    received = [along_y(grad_pieces[Y_SIZE + step], step) for step in range(1, Y_SIZE)]
    partial = grad_pieces[Y_SIZE] + sum(piece.astype(f32) for piece in received)
    received = [along_y(grad_pieces[step], step) for step in range(1, Y_SIZE)]
    grads = pl.pallas_call(
        sum_kernel,
        in_specs=[VMEM] * 5,
        out_shape=shape((tm, 2 * shard, width), bf16),
        compiler_params=vmem_params(),
        cost_estimate=pl.CostEstimate(flops=10000000000, bytes_accessed=2 * 2**20, transcendentals=0),
        name="sum_blocks",
    )(grad_pieces[0], *received, across_x(partial.astype(bf16)))

    sent = pl.pallas_call(
        input_kernel,
        out_shape=shape((tm, 3 * per_peer, width // 2), bf16),
        in_specs=[HBM] * 7 + [VMEM],
        scratch_shapes=[
            pltpu.VMEM(got.shape, bf16),
            pltpu.VMEM((rows, 3 * HALF), bf16),
            pltpu.VMEM((rows, 3 * HALF), bf16),
            pltpu.VMEM((rows, HALF), bf16),
            pltpu.VMEM((rows, HALF), bf16),
            pltpu.VMEM((width, 3 * HALF), bf16),
            pltpu.VMEM((width, 3 * HALF), bf16),
            pltpu.SemaphoreType.DMA((7,)),
        ],
        compiler_params=vmem_params(),
        cost_estimate=pl.CostEstimate(flops=10**9, bytes_accessed=6 * 2**20, transcendentals=0),
        name="input_gradient",
    )(got, d_packed, dp_other, mixed, mixed_other, w_mine, w_other, gain_row)
    got = swap(sent.reshape(-1, width // 2), TM).reshape(sent.shape)
    grads, got = lax.optimization_barrier((grads, got))
    local = shape(frames_in.shape[1:], bf16)
    result, grad_in = pl.pallas_call(
        home_kernel,
        in_specs=[HBM] * 4,
        out_specs=(HBM,) * 2,
        out_shape=(local,) * 2,
        scratch_shapes=[
            pltpu.VMEM(sent.shape, bf16),
            pltpu.VMEM(local.shape, bf16),
            pltpu.VMEM((width, HALF), bf16),
            pltpu.VMEM((width, HALF), bf16),
            pltpu.VMEM(local.shape, bf16),
            pltpu.VMEM(local.shape, bf16),
            pltpu.SemaphoreType.DMA((4,)),
        ],
        compiler_params=vmem_params(),
        cost_estimate=pl.CostEstimate(flops=3 * 10**8, bytes_accessed=4 * 2**20, transcendentals=0),
        name="home",
    )(got, frames_in[0], w_mine, w_other)

    grads = swap(grads.reshape(-1, width), TM)
    grads, result, grad_in = lax.optimization_barrier((grads, result, grad_in))
    total = jnp.sum(grads.reshape(tm, 2, shard, width).astype(f32), axis=0)
    keep = lax.dynamic_index_in_dim(total, core, 0, keepdims=False)
    recv = exchange(lax.dynamic_index_in_dim(total, 1 - core, 0, keepdims=False))
    low = jnp.where(first, keep, recv).reshape(shard, 4, 1, HALF)
    high = jnp.where(first, recv, keep).reshape(shard, 4, 1, HALF)
    whole = jnp.concatenate([low, high], axis=2)
    grad_qkv = whole[:, :3].reshape(shard, 6 * HALF)
    grad_out = whole[:, 3].reshape(shard, 2 * HALF).T
    own_row = lax.axis_index(DP + TM) * shard
    grad_gain = jnp.sum(w_qkv.astype(f32) * grad_qkv, axis=1) / lax.dynamic_slice_in_dim(gain, own_row, shard)
    return (result[None], grad_in[None], grad_qkv, grad_out, grad_gain)


def solution(mesh):
    fine = Mesh(mesh.devices.reshape(Y_SIZE, XH_SIZE, 2, 2, 8), DP + TM)
    in_specs = (
        P(DP, TM, None, None),
        P(),
        P(DP + TM, None),
        P(None, DP + TM),
        P(DP, TM, None, None),
    )
    out_specs = (
        P(DP, TM, None, None),
        P(DP, TM, None, None),
        P(DP + TM, None),
        P(None, DP + TM),
        P(DP + TM),
    )
    return jax.shard_map(body, mesh=fine, in_specs=in_specs, out_specs=out_specs, check_vma=False)
```

```python
import functools

import jax
import jax.numpy as jnp
from jax import lax
from jax.experimental import pallas as pl
from jax.experimental.pallas import tpu as pltpu
from jax.sharding import Mesh, PartitionSpec as P

DP = ("y", "xh", "core")
TM = ("xl", "z")
Y_SIZE, XH_SIZE, TM_SIZE = 4, 2, 16

D = 1024
DH = 64
HALF = 256
norm_eps = 1e-05
f32 = jnp.float32
bf16 = jnp.bfloat16

NN = (((1,), (0,)), ((), ()))
NT = (((1,), (1,)), ((), ()))
TN = (((0,), (0,)), ((), ()))

VMEM = pl.BlockSpec(memory_space=pltpu.VMEM)
ANY = pl.BlockSpec(memory_space=pl.ANY)


def mm(a, b, dims):
    return lax.dot_general(a, b, dims, preferred_element_type=f32)


def layer_stats(features):
    wide = features.astype(f32)
    centred = wide - jnp.mean(wide, axis=-1, keepdims=True)
    inv_std = lax.rsqrt(jnp.mean(centred * centred, axis=-1, keepdims=True) + norm_eps)
    return centred * inv_std, inv_std


def pack_weights_kernel(w_qkv_ref, w_out_ref, out_ref):
    qkv, out = w_qkv_ref[...].astype(f32), w_out_ref[...].astype(f32)
    halves = []
    for half in range(2):
        parts = [qkv[:, (2 * part + half) * HALF : (2 * part + half + 1) * HALF] for part in range(3)]
        halves.append(jnp.concatenate(parts + [out[:, half * HALF : (half + 1) * HALF]], axis=1))
    both = jnp.concatenate(halves, axis=0)
    out_ref[...] = jnp.broadcast_to(both[None], out_ref.shape).astype(bf16)


def fetch(pairs, sems, first=0):
    copies = [pltpu.make_async_copy(src, dst, sems.at[first + i]) for i, (src, dst) in enumerate(pairs)]
    for copy in copies:
        copy.start()
    return copies


def wait_all(copies):
    for copy in copies:
        copy.wait()


CHUNK = 64


def sample(patches, got, gain_ref, weights, normed, mixed, dpacked, slots, before_weights):
    scores, d_probs, low_probs, d_scores = slots
    rows = normed.shape[0]
    per_peer = got.shape[1] // 2
    group = 4
    for peer in range(0, got.shape[0], group):
        features = got[peer : peer + group, :per_peer, :].reshape(group * per_peer, D)
        normal_x, _ = layer_stats(features)
        normed[peer * per_peer : (peer + group) * per_peer, :] = (normal_x * gain_ref[...]).astype(bf16)
    before_weights()
    packed = mm(normed[...], weights[:, : 3 * HALF], NN).astype(bf16)
    d_mixed = mm(got[:, per_peer:, :].reshape(rows, D), weights[:, 3 * HALF :], NN).astype(bf16)
    row_patch = lax.broadcasted_iota(jnp.int32, (CHUNK, rows), 0) % patches
    col_patch = lax.broadcasted_iota(jnp.int32, (CHUNK, rows), 1) % patches
    bias = jnp.where(row_patch == col_patch, 0.0, -1e30)
    low_half = lax.broadcasted_iota(jnp.int32, (rows, 2 * DH), 1) < DH
    zero = jnp.zeros((rows, 2 * DH), bf16)
    heads = HALF // DH

    def part(index, head):
        lo = index * HALF + head // 2 * 2 * DH
        return packed[:, lo : lo + 2 * DH]

    def d_part(head):
        lo = head // 2 * 2 * DH
        return d_mixed[:, lo : lo + 2 * DH]

    for head in range(heads):
        own = low_half if head % 2 == 0 else jnp.logical_not(low_half)
        query = jnp.where(own, part(0, head) * DH ** (-0.5), zero)
        scores[head] = mm(query, part(1, head), NT)
        d_probs[head] = mm(jnp.where(own, d_part(head), zero), part(2, head), NT)
    for pair in range(heads // 2):
        outs = []
        for head in (2 * pair, 2 * pair + 1):
            for at in range(0, rows, CHUNK):
                score = scores[head, at : at + CHUNK, :] + bias
                expo = jnp.exp(score - jnp.max(score, axis=-1, keepdims=True))
                prob = expo * (1.0 / jnp.sum(expo, axis=-1, keepdims=True))
                low_probs[head, at : at + CHUNK, :] = prob.astype(bf16)
                d_prob = d_probs[head, at : at + CHUNK, :]
                inner = jnp.sum(d_prob * prob, axis=-1, keepdims=True)
                d_scores[head, at : at + CHUNK, :] = (prob * (d_prob - inner)).astype(bf16)
            outs.append(
                (
                    mm(low_probs[head], part(2, head), NN),
                    mm(d_scores[head], part(1, head), NN) * DH ** (-0.5),
                    mm(d_scores[head], part(0, head), TN) * DH ** (-0.5),
                    mm(low_probs[head], d_part(head), TN),
                )
            )
        outs = [jnp.where(low_half, low, high).astype(bf16) for low, high in zip(*outs)]
        lo = pair * 2 * DH
        mixed[:, lo : lo + 2 * DH] = outs[0]
        for index in range(3):
            at = index * HALF + lo
            dpacked[:, at : at + 2 * DH] = outs[1 + index]


def block_of(step, side):
    y, xh = lax.axis_index("y"), lax.axis_index("xh")
    return lax.rem(y + step + Y_SIZE, Y_SIZE) * XH_SIZE + lax.rem(xh + side, XH_SIZE)


def arrived_kernel(*refs):
    refs[-1][...] = jnp.zeros_like(refs[-1])


def layer_kernel(patches, got_own_ref, got_other_ref, gain_ref, token_ref, *refs):
    pieces, outs, grad_refs, scratch = refs[:8], refs[8:13], refs[13:21], refs[21:]
    w_ref, mixed_own_ref, dnormed_own_ref, mixed_other_ref, dnormed_other_ref = outs
    got, weights, normed, mixed, dpacked, dnormed, grads, own, peers = scratch[:9]
    slots, (sems, out_sems) = scratch[9:13], scratch[13:]
    copies = fetch([(got_own_ref, got.at[0])], sems)
    block = own.shape[1]
    places = [block_of(-(i % Y_SIZE), i // Y_SIZE) for i in range(8)]
    starts = [pl.multiple_of(place * block, block) for place in places]
    copies += fetch([(p, weights.at[pl.ds(at, block), :]) for p, at in zip(pieces, starts)], sems, 1)
    copies += fetch([(got_other_ref, got.at[1])], sems, 9)
    results = []
    per_peer = got.shape[2] // 2

    def before_weights():
        wait_all(copies[1:9])
        results.extend(fetch([(weights.at[:, 3 * HALF :], w_ref)], out_sems))

    copies[0].wait()
    arguments = (got.at[0], gain_ref, weights, normed.at[0], mixed.at[0], dpacked.at[0])
    sample(patches, *arguments, slots, before_weights)
    dnormed[0] = mm(dpacked[0], weights[:, : 3 * HALF], NT)
    results += fetch([(mixed.at[0], mixed_own_ref), (dnormed.at[0], dnormed_own_ref)], out_sems, 1)
    copies[9].wait()
    arguments = (got.at[1], gain_ref, weights, normed.at[1], mixed.at[1], dpacked.at[1])
    sample(patches, *arguments, slots, lambda: None)
    dnormed[1] = mm(dpacked[1], weights[:, : 3 * HALF], NT)
    results += fetch([(mixed.at[1], mixed_other_ref), (dnormed.at[1], dnormed_other_ref)], out_sems, 3)
    rows = normed.shape[1]
    pair_rows = 2 * block
    all_dpacked = dpacked[...].reshape(2 * rows, 3 * HALF)
    all_mixed = mixed[...].reshape(2 * rows, HALF)
    y, xh = lax.axis_index("y"), lax.axis_index("xh")
    for step in (1, 2, 3, 0):
        start = pl.multiple_of(lax.rem(y + step, Y_SIZE) * pair_rows, pair_rows)
        columns = pl.ds(start, pair_rows)
        grads[:, : 3 * HALF] = mm(normed[:, :, columns].reshape(2 * rows, pair_rows), all_dpacked, TN)
        grads[:, 3 * HALF :] = mm(got[:, :, per_peer:, columns].reshape(2 * rows, pair_rows), all_mixed, TN)
        for side in range(XH_SIZE):
            start = pl.multiple_of(lax.rem(xh + side, XH_SIZE) * block, block)
            slot = own.at[side] if step == 0 else peers.at[side * (Y_SIZE - 1) + step - 1]
            slot[...] = grads[pl.ds(start, block), :].astype(slot.dtype)
            results += fetch([(slot, grad_refs[side * Y_SIZE + step])], out_sems, len(results))
    wait_all(results)


def input_kernel(got_ref, mine_ref, mixed_ref, other, mixed_other, gain_ref, out_ref, got, mine, mixed, out, sems):
    copies = fetch([(got_ref, got), (mine_ref, mine), (mixed_ref, mixed)], sems)
    peers, per_peer = got.shape[0], got.shape[1] // 2
    wait_all(copies)
    results = []
    group = 4
    half = (group, per_peer, D // 2)
    for peer in range(0, peers, group):
        at = slice(peer, peer + group)
        rows = slice(peer * per_peer, (peer + group) * per_peer)
        normal_x, inv_std = layer_stats(got[at, :per_peer, :].reshape(group * per_peer, D))
        scaled = (mine[rows, :] + other[rows, :]).astype(bf16).astype(f32) * gain_ref[...]
        d_input = inv_std * (
            scaled
            - jnp.mean(scaled, axis=-1, keepdims=True)
            - normal_x * jnp.mean(scaled * normal_x, axis=-1, keepdims=True)
        )
        grad_in = (got[at, per_peer:, :].reshape(group * per_peer, D).astype(f32) + d_input).astype(bf16)
        out[at, :per_peer, :] = grad_in[:, : D // 2].reshape(half)
        out[at, per_peer : 2 * per_peer, :] = grad_in[:, D // 2 :].reshape(half)
        out[at, 2 * per_peer :, :HALF] = mixed[rows, :].reshape(group, per_peer, HALF)
        out[at, 2 * per_peer :, HALF:] = mixed_other[rows, :].reshape(group, per_peer, HALF)
        results += fetch([(out.at[at], out_ref.at[at])], sems, 3 + len(results))
    wait_all(results)


def sum_kernel(own_ref, a_ref, b_ref, c_ref, across_ref, out_ref):
    total = own_ref[...] + a_ref[...].astype(f32) + b_ref[...].astype(f32) + c_ref[...].astype(f32)
    total = total + across_ref[...].astype(f32)
    shard = 4
    low, high = (total.reshape(2, -1, 2 * shard, D)[core] for core in range(2))
    top = lax.broadcasted_iota(jnp.int32, low.shape, 1) < shard
    even = jnp.where(top, low, pltpu.roll(high, shard, 1))
    odd = jnp.where(top, pltpu.roll(low, shard, 1), high)
    out_ref[...] = jnp.stack([even, odd], axis=1).reshape(out_ref.shape).astype(bf16)


def home_kernel(got_ref, x_ref, w_mine_ref, w_other_ref, result_ref, grad_ref, got, x, w_mine, w_other, result, grad, sems):
    wait_all(
        fetch(
            [(got_ref, got), (x_ref, x), (w_mine_ref, w_mine), (w_other_ref, w_other)],
            sems,
        )
    )
    peers, _, width = got.shape
    frames, count, _ = x.shape
    patches = count // peers
    per_peer = frames * patches

    def by_frame(part):
        wide = got[:, part * per_peer : (part + 1) * per_peer, :].astype(f32)
        wide = wide.reshape(peers, frames, patches, width)
        return [wide[:, f].reshape(count, width).astype(bf16) for f in range(frames)]

    low, high, heads = by_frame(0), by_frame(1), by_frame(2)
    for f in range(frames):
        grad[f, :, :width] = low[f]
        grad[f, :, width:] = high[f]
    results = fetch([(grad, grad_ref)], sems)
    for f in range(frames):
        projected = mm(heads[f][:, :HALF], w_mine[...], NT) + mm(heads[f][:, HALF:], w_other[...], NT)
        result[f] = (x[f].astype(f32) + projected).astype(bf16)
    wait_all(results + fetch([(result, result_ref)], sems, 1))


def vmem_params(mib=60):
    return pltpu.CompilerParams(vmem_limit_bytes=mib * 2**20)


def exchange(value):
    return lax.ppermute(value, "core", [(0, 1), (1, 0)])


def swap(value, axes):
    return lax.all_to_all(value, axes, split_axis=0, concat_axis=0, tiled=True)


def along_y(value, step):
    return lax.ppermute(value, "y", [(i, (i + step) % Y_SIZE) for i in range(Y_SIZE)])


def across_x(value):
    return lax.ppermute(value, "xh", [(0, 1), (1, 0)])


def body(frames_in, gain, w_qkv, w_out, out_grad):
    _, frames, patch_count, width = frames_in.shape
    tm = TM_SIZE
    patches = patch_count // tm
    per_peer = frames * patches
    rows = tm * per_peer
    shard = w_qkv.shape[0]
    core = lax.axis_index("core")
    first = core == 0
    gain_row = gain.reshape(1, width)

    def by_patch(value):
        value = value.reshape(frames, tm, patches, width).transpose(1, 0, 2, 3)
        return value.reshape(tm, per_peer, width)

    w_parts = pl.pallas_call(
        pack_weights_kernel,
        out_shape=jax.ShapeDtypeStruct((tm, 2 * shard, width), bf16),
        in_specs=[VMEM] * 2,
        compiler_params=vmem_params(),
        cost_estimate=pl.CostEstimate(flops=0, bytes_accessed=2**18, transcendentals=0),
        name="pack_weights",
    )(w_qkv, w_out.T)
    w_got = swap(w_parts.reshape(-1, width), TM).reshape(tm, 2, shard, width)

    w_keep = lax.dynamic_index_in_dim(w_got, core, 1, keepdims=False).reshape(tm * shard, width)
    w_send = lax.dynamic_index_in_dim(w_got, 1 - core, 1, keepdims=False).reshape(tm * shard, width)
    w_recv = exchange(w_send)
    w_block = jnp.concatenate(
        [jnp.where(first, w_keep, w_recv), jnp.where(first, w_recv, w_keep)], axis=0
    )
    block = w_block.shape[0]

    sent = jnp.concatenate([by_patch(frames_in), by_patch(out_grad)], axis=1)
    sent, w_block = lax.optimization_barrier((sent, w_block))
    got = swap(sent.reshape(-1, width), TM).reshape(tm, 2 * per_peer, width)

    pieces = []
    for part in (w_block, across_x(w_block)):
        pieces += [part] + [along_y(part, step) for step in range(1, Y_SIZE)]
    got_other = exchange(got)

    shape = jax.ShapeDtypeStruct
    token = pl.pallas_call(
        arrived_kernel,
        in_specs=[ANY] * 8,
        out_specs=VMEM,
        out_shape=shape((8, 128), f32),
        compiler_params=vmem_params(),
        cost_estimate=pl.CostEstimate(flops=2 * 10**10, bytes_accessed=4 * 2**20, transcendentals=0),
        name="arrived",
    )(*pieces)

    sample_shapes = (shape((rows, HALF), bf16), shape((rows, width), f32))
    half_shape, own_shape = shape((block, width), bf16), shape((block, width), f32)
    w_mine, mixed, d_normed, mixed_2, d_normed_2, *grad_pieces = pl.pallas_call(
        functools.partial(layer_kernel, patches),
        in_specs=[ANY, ANY, VMEM, VMEM] + [ANY] * 8,
        out_specs=(ANY,) * 13,
        out_shape=(shape((width, HALF), bf16),)
        + sample_shapes * 2 + ((own_shape,) + (half_shape,) * (Y_SIZE - 1)) * 2,
        scratch_shapes=[
            pltpu.VMEM((2,) + got.shape, bf16),
            pltpu.VMEM((width, width), bf16),
            pltpu.VMEM((2, rows, width), bf16),
            pltpu.VMEM((2, rows, HALF), bf16),
            pltpu.VMEM((2, rows, 3 * HALF), bf16),
            pltpu.VMEM((2, rows, width), f32),
            pltpu.VMEM((2 * block, width), f32),
            pltpu.VMEM((2, block, width), f32),
            pltpu.VMEM((6, block, width), bf16),
            pltpu.VMEM((HALF // DH, rows, rows), f32),
            pltpu.VMEM((HALF // DH, rows, rows), f32),
            pltpu.VMEM((HALF // DH, rows, rows), bf16),
            pltpu.VMEM((HALF // DH, rows, rows), bf16),
            pltpu.SemaphoreType.DMA((10,)),
            pltpu.SemaphoreType.DMA((13,)),
        ],
        compiler_params=vmem_params(),
        cost_estimate=pl.CostEstimate(flops=3 * 10**10, bytes_accessed=10 * 2**20, transcendentals=2**19),
        name="layer",
    )(got, got_other, gain_row, token, *pieces)
    w_other = exchange(w_mine)
    d_normed_other = exchange(d_normed_2)
    mixed_other = exchange(mixed_2)

    received = [along_y(grad_pieces[Y_SIZE + step], step) for step in range(1, Y_SIZE)]
    partial = grad_pieces[Y_SIZE] + sum(piece.astype(f32) for piece in received)
    received = [along_y(grad_pieces[step], step) for step in range(1, Y_SIZE)]
    grads = pl.pallas_call(
        sum_kernel,
        in_specs=[VMEM] * 5,
        out_shape=shape((tm, 2 * shard, width), bf16),
        compiler_params=vmem_params(8),
        cost_estimate=pl.CostEstimate(flops=10**10, bytes_accessed=2 * 2**20, transcendentals=0),
        name="sum_blocks",
    )(grad_pieces[0], *received, across_x(partial.astype(bf16)))

    sent = pl.pallas_call(
        input_kernel,
        out_shape=shape((tm, 3 * per_peer, width // 2), bf16),
        in_specs=[ANY] * 3 + [VMEM] * 3,
        out_specs=ANY,
        scratch_shapes=[
            pltpu.VMEM(got.shape, bf16),
            pltpu.VMEM((rows, width), f32),
            pltpu.VMEM((rows, HALF), bf16),
            pltpu.VMEM((tm, 3 * per_peer, width // 2), bf16),
            pltpu.SemaphoreType.DMA((11,)),
        ],
        compiler_params=vmem_params(56),
        cost_estimate=pl.CostEstimate(flops=10**9, bytes_accessed=6 * 2**20, transcendentals=0),
        name="input_gradient",
    )(got, d_normed, mixed, d_normed_other, mixed_other, gain_row)
    got = swap(sent.reshape(-1, width // 2), TM).reshape(sent.shape)
    grads, got = lax.optimization_barrier((grads, got))
    local = shape(frames_in.shape[1:], bf16)
    result, grad_in = pl.pallas_call(
        home_kernel,
        in_specs=[ANY] * 4,
        out_specs=(ANY,) * 2,
        out_shape=(local,) * 2,
        scratch_shapes=[
            pltpu.VMEM(sent.shape, bf16),
            pltpu.VMEM(local.shape, bf16),
            pltpu.VMEM((width, HALF), bf16),
            pltpu.VMEM((width, HALF), bf16),
            pltpu.VMEM(local.shape, bf16),
            pltpu.VMEM(local.shape, bf16),
            pltpu.SemaphoreType.DMA((4,)),
        ],
        compiler_params=vmem_params(),
        cost_estimate=pl.CostEstimate(flops=3 * 10**8, bytes_accessed=4 * 2**20, transcendentals=0),
        name="home",
    )(got, frames_in[0], w_mine, w_other)

    grads = swap(grads.reshape(-1, width), TM)
    grads, result, grad_in = lax.optimization_barrier((grads, result, grad_in))
    total = jnp.sum(grads.reshape(tm, 2, shard, width).astype(f32), axis=0)
    keep = lax.dynamic_index_in_dim(total, core, 0, keepdims=False)
    recv = exchange(lax.dynamic_index_in_dim(total, 1 - core, 0, keepdims=False))
    low = jnp.where(first, keep, recv).reshape(shard, 4, 1, HALF)
    high = jnp.where(first, recv, keep).reshape(shard, 4, 1, HALF)
    whole = jnp.concatenate([low, high], axis=2)
    grad_qkv = whole[:, :3].reshape(shard, 6 * HALF)
    grad_out = whole[:, 3].reshape(shard, 2 * HALF).T
    own_row = lax.axis_index(DP + TM) * shard
    grad_gain = jnp.sum(w_qkv.astype(f32) * grad_qkv, axis=1) / lax.dynamic_slice_in_dim(gain, own_row, shard)
    return (result[None], grad_in[None], grad_qkv, grad_out, grad_gain)


def solution(mesh):
    fine = Mesh(mesh.devices.reshape(Y_SIZE, XH_SIZE, 2, 2, 8), DP + TM)
    in_specs = (
        P(DP, TM, None, None),
        P(),
        P(DP + TM, None),
        P(None, DP + TM),
        P(DP, TM, None, None),
    )
    out_specs = (
        P(DP, TM, None, None),
        P(DP, TM, None, None),
        P(DP + TM, None),
        P(None, DP + TM),
        P(DP + TM),
    )
    return jax.shard_map(body, mesh=fine, in_specs=in_specs, out_specs=out_specs, check_vma=False)
```

```python
import functools

import jax
import jax.numpy as jnp
from jax import lax
from jax.experimental import pallas as pl
from jax.experimental.pallas import tpu as pltpu
from jax.sharding import Mesh, PartitionSpec as P

DP = ("y", "xh", "core")
TM = ("xl", "z")
Y_SIZE, XH_SIZE, TM_SIZE = 4, 2, 16

D = 1024
DH = 64
HALF = 256
norm_eps = 1e-05
f32 = jnp.float32
bf16 = jnp.bfloat16

NN = (((1,), (0,)), ((), ()))
NT = (((1,), (1,)), ((), ()))
TN = (((0,), (0,)), ((), ()))

VMEM = pl.BlockSpec(memory_space=pltpu.VMEM)
ANY = pl.BlockSpec(memory_space=pl.ANY)


def mm(a, b, dims):
    return lax.dot_general(a, b, dims, preferred_element_type=f32)


def layer_stats(features):
    wide = features.astype(f32)
    centred = wide - jnp.mean(wide, axis=-1, keepdims=True)
    inv_std = lax.rsqrt(jnp.mean(centred * centred, axis=-1, keepdims=True) + norm_eps)
    return centred * inv_std, inv_std


def pack_weights_kernel(w_qkv_ref, w_out_ref, out_ref):
    qkv, out = w_qkv_ref[...].astype(f32), w_out_ref[...].astype(f32)
    halves = []
    for half in range(2):
        parts = [qkv[:, (2 * part + half) * HALF : (2 * part + half + 1) * HALF] for part in range(3)]
        halves.append(jnp.concatenate(parts + [out[:, half * HALF : (half + 1) * HALF]], axis=1))
    both = jnp.concatenate(halves, axis=0)
    out_ref[...] = jnp.broadcast_to(both[None], out_ref.shape).astype(bf16)


def fetch(pairs, sems, first=0):
    copies = [pltpu.make_async_copy(src, dst, sems.at[first + i]) for i, (src, dst) in enumerate(pairs)]
    for copy in copies:
        copy.start()
    return copies


def wait_all(copies):
    for copy in copies:
        copy.wait()


CHUNK = 64


def sample(patches, got, gain_ref, weights, normed, mixed, dpacked, slots, before_weights):
    scores, d_probs, low_probs, d_scores = slots
    rows = normed.shape[0]
    per_peer = got.shape[1] // 2
    group = 4
    for peer in range(0, got.shape[0], group):
        features = got[peer : peer + group, :per_peer, :].reshape(group * per_peer, D)
        normal_x, _ = layer_stats(features)
        normed[peer * per_peer : (peer + group) * per_peer, :] = (normal_x * gain_ref[...]).astype(bf16)
    before_weights()
    packed = mm(normed[...], weights[:, : 3 * HALF], NN).astype(bf16)
    d_mixed = mm(got[:, per_peer:, :].reshape(rows, D), weights[:, 3 * HALF :], NN).astype(bf16)
    row_patch = lax.broadcasted_iota(jnp.int32, (CHUNK, rows), 0) % patches
    col_patch = lax.broadcasted_iota(jnp.int32, (CHUNK, rows), 1) % patches
    bias = jnp.where(row_patch == col_patch, 0.0, -1e30)
    low_half = lax.broadcasted_iota(jnp.int32, (rows, 2 * DH), 1) < DH
    zero = jnp.zeros((rows, 2 * DH), bf16)
    heads = HALF // DH

    def part(index, head):
        lo = index * HALF + head // 2 * 2 * DH
        return packed[:, lo : lo + 2 * DH]

    def d_part(head):
        lo = head // 2 * 2 * DH
        return d_mixed[:, lo : lo + 2 * DH]

    for head in range(heads):
        own = low_half if head % 2 == 0 else jnp.logical_not(low_half)
        query = jnp.where(own, part(0, head) * DH ** (-0.5), zero)
        scores[head] = mm(query, part(1, head), NT)
        d_probs[head] = mm(jnp.where(own, d_part(head), zero), part(2, head), NT)
    for pair in range(heads // 2):
        outs = []
        for head in (2 * pair, 2 * pair + 1):
            for at in range(0, rows, CHUNK):
                score = scores[head, at : at + CHUNK, :] + bias
                expo = jnp.exp(score - jnp.max(score, axis=-1, keepdims=True))
                prob = expo * (1.0 / jnp.sum(expo, axis=-1, keepdims=True))
                low_probs[head, at : at + CHUNK, :] = prob.astype(bf16)
                d_prob = d_probs[head, at : at + CHUNK, :]
                inner = jnp.sum(d_prob * prob, axis=-1, keepdims=True)
                d_scores[head, at : at + CHUNK, :] = (prob * (d_prob - inner)).astype(bf16)
            outs.append(
                (
                    mm(low_probs[head], part(2, head), NN),
                    mm(d_scores[head], part(1, head), NN) * DH ** (-0.5),
                    mm(d_scores[head], part(0, head), TN) * DH ** (-0.5),
                    mm(low_probs[head], d_part(head), TN),
                )
            )
        outs = [jnp.where(low_half, low, high).astype(bf16) for low, high in zip(*outs)]
        lo = pair * 2 * DH
        mixed[:, lo : lo + 2 * DH] = outs[0]
        for index in range(3):
            at = index * HALF + lo
            dpacked[:, at : at + 2 * DH] = outs[1 + index]


def block_of(step, side):
    y, xh = lax.axis_index("y"), lax.axis_index("xh")
    return lax.rem(y + step + Y_SIZE, Y_SIZE) * XH_SIZE + lax.rem(xh + side, XH_SIZE)


def arrived_kernel(*refs):
    refs[-1][...] = jnp.zeros_like(refs[-1])


def layer_kernel(patches, got_own_ref, got_other_ref, gain_ref, token_ref, *refs):
    pieces, outs, grad_refs, scratch = refs[:8], refs[8:13], refs[13:21], refs[21:]
    w_ref, mixed_own_ref, dnormed_own_ref, mixed_other_ref, dnormed_other_ref = outs
    got, weights, normed, mixed, dpacked, dnormed, grads, own, peers = scratch[:9]
    slots, (sems, out_sems) = scratch[9:13], scratch[13:]
    copies = fetch([(got_own_ref, got.at[0])], sems)
    block = own.shape[1]
    places = [block_of(-(i % Y_SIZE), i // Y_SIZE) for i in range(8)]
    starts = [pl.multiple_of(place * block, block) for place in places]
    copies += fetch([(p, weights.at[pl.ds(at, block), :]) for p, at in zip(pieces, starts)], sems, 1)
    copies += fetch([(got_other_ref, got.at[1])], sems, 9)
    results = []
    per_peer = got.shape[2] // 2

    def before_weights():
        wait_all(copies[1:9])
        results.extend(fetch([(weights.at[:, 3 * HALF :], w_ref)], out_sems))

    copies[0].wait()
    arguments = (got.at[0], gain_ref, weights, normed.at[0], mixed.at[0], dpacked.at[0])
    sample(patches, *arguments, slots, before_weights)
    dnormed[0] = mm(dpacked[0], weights[:, : 3 * HALF], NT)
    results += fetch([(mixed.at[0], mixed_own_ref), (dnormed.at[0], dnormed_own_ref)], out_sems, 1)
    copies[9].wait()
    arguments = (got.at[1], gain_ref, weights, normed.at[1], mixed.at[1], dpacked.at[1])
    sample(patches, *arguments, slots, lambda: None)
    dnormed[1] = mm(dpacked[1], weights[:, : 3 * HALF], NT)
    results += fetch([(mixed.at[1], mixed_other_ref), (dnormed.at[1], dnormed_other_ref)], out_sems, 3)
    rows = normed.shape[1]
    pair_rows = 2 * block
    all_dpacked = dpacked[...].reshape(2 * rows, 3 * HALF)
    all_mixed = mixed[...].reshape(2 * rows, HALF)
    y, xh = lax.axis_index("y"), lax.axis_index("xh")
    for step in (1, 2, 3, 0):
        start = pl.multiple_of(lax.rem(y + step, Y_SIZE) * pair_rows, pair_rows)
        columns = pl.ds(start, pair_rows)
        grads[:, : 3 * HALF] = mm(normed[:, :, columns].reshape(2 * rows, pair_rows), all_dpacked, TN)
        grads[:, 3 * HALF :] = mm(got[:, :, per_peer:, columns].reshape(2 * rows, pair_rows), all_mixed, TN)
        for side in range(XH_SIZE):
            start = pl.multiple_of(lax.rem(xh + side, XH_SIZE) * block, block)
            slot = own.at[side] if step == 0 else peers.at[side * (Y_SIZE - 1) + step - 1]
            slot[...] = grads[pl.ds(start, block), :].astype(slot.dtype)
            results += fetch([(slot, grad_refs[side * Y_SIZE + step])], out_sems, len(results))
    wait_all(results)


def input_kernel(got_ref, mine_ref, mixed_ref, other, mixed_other, gain_ref, out_ref, got, mine, mixed, out, sems):
    copies = fetch([(got_ref, got), (mine_ref, mine), (mixed_ref, mixed)], sems)
    peers, per_peer = got.shape[0], got.shape[1] // 2
    wait_all(copies)
    results = []
    group = 4
    half = (group, per_peer, D // 2)
    for peer in range(0, peers, group):
        at = slice(peer, peer + group)
        rows = slice(peer * per_peer, (peer + group) * per_peer)
        normal_x, inv_std = layer_stats(got[at, :per_peer, :].reshape(group * per_peer, D))
        scaled = (mine[rows, :] + other[rows, :]).astype(bf16).astype(f32) * gain_ref[...]
        d_input = inv_std * (
            scaled
            - jnp.mean(scaled, axis=-1, keepdims=True)
            - normal_x * jnp.mean(scaled * normal_x, axis=-1, keepdims=True)
        )
        grad_in = (got[at, per_peer:, :].reshape(group * per_peer, D).astype(f32) + d_input).astype(bf16)
        out[at, :per_peer, :] = grad_in[:, : D // 2].reshape(half)
        out[at, per_peer : 2 * per_peer, :] = grad_in[:, D // 2 :].reshape(half)
        out[at, 2 * per_peer :, :HALF] = mixed[rows, :].reshape(group, per_peer, HALF)
        out[at, 2 * per_peer :, HALF:] = mixed_other[rows, :].reshape(group, per_peer, HALF)
        results += fetch([(out.at[at], out_ref.at[at])], sems, 3 + len(results))
    wait_all(results)


def sum_kernel(own_ref, a_ref, b_ref, c_ref, across_ref, out_ref):
    total = own_ref[...] + a_ref[...].astype(f32) + b_ref[...].astype(f32) + c_ref[...].astype(f32)
    total = total + across_ref[...].astype(f32)
    shard = 4
    low, high = (total.reshape(2, -1, 2 * shard, D)[core] for core in range(2))
    top = lax.broadcasted_iota(jnp.int32, low.shape, 1) < shard
    even = jnp.where(top, low, pltpu.roll(high, shard, 1))
    odd = jnp.where(top, pltpu.roll(low, shard, 1), high)
    out_ref[...] = jnp.stack([even, odd], axis=1).reshape(out_ref.shape).astype(bf16)


def home_kernel(got_ref, x_ref, w_mine_ref, w_other_ref, result_ref, grad_ref, got, x, w_mine, w_other, result, grad, sems):
    wait_all(
        fetch(
            [(got_ref, got), (x_ref, x), (w_mine_ref, w_mine), (w_other_ref, w_other)],
            sems,
        )
    )
    peers, _, width = got.shape
    frames, count, _ = x.shape
    patches = count // peers
    per_peer = frames * patches

    def by_frame(part):
        wide = got[:, part * per_peer : (part + 1) * per_peer, :].astype(f32)
        wide = wide.reshape(peers, frames, patches, width)
        return [wide[:, f].reshape(count, width).astype(bf16) for f in range(frames)]

    low, high, heads = by_frame(0), by_frame(1), by_frame(2)
    for f in range(frames):
        grad[f, :, :width] = low[f]
        grad[f, :, width:] = high[f]
    results = fetch([(grad, grad_ref)], sems)
    for f in range(frames):
        projected = mm(heads[f][:, :HALF], w_mine[...], NT) + mm(heads[f][:, HALF:], w_other[...], NT)
        result[f] = (x[f].astype(f32) + projected).astype(bf16)
    wait_all(results + fetch([(result, result_ref)], sems, 1))


def vmem_params(mib=60):
    return pltpu.CompilerParams(vmem_limit_bytes=mib * 2**20)


def exchange(value):
    return lax.ppermute(value, "core", [(0, 1), (1, 0)])


def swap(value, axes):
    return lax.all_to_all(value, axes, split_axis=0, concat_axis=0, tiled=True)


def along_y(value, step):
    return lax.ppermute(value, "y", [(i, (i + step) % Y_SIZE) for i in range(Y_SIZE)])


def across_x(value):
    return lax.ppermute(value, "xh", [(0, 1), (1, 0)])


def body(frames_in, gain, w_qkv, w_out, out_grad):
    _, frames, patch_count, width = frames_in.shape
    tm = TM_SIZE
    patches = patch_count // tm
    per_peer = frames * patches
    rows = tm * per_peer
    shard = w_qkv.shape[0]
    core = lax.axis_index("core")
    first = core == 0
    gain_row = gain.reshape(1, width)

    def by_patch(value):
        value = value.reshape(frames, tm, patches, width).transpose(1, 0, 2, 3)
        return value.reshape(tm, per_peer, width)

    w_parts = pl.pallas_call(
        pack_weights_kernel,
        out_shape=jax.ShapeDtypeStruct((tm, 2 * shard, width), bf16),
        in_specs=[VMEM] * 2,
        compiler_params=vmem_params(),
        cost_estimate=pl.CostEstimate(flops=0, bytes_accessed=2**18, transcendentals=0),
        name="pack_weights",
    )(w_qkv, w_out.T)
    w_got = swap(w_parts.reshape(-1, width), TM).reshape(tm, 2, shard, width)

    w_keep = lax.dynamic_index_in_dim(w_got, core, 1, keepdims=False).reshape(tm * shard, width)
    w_send = lax.dynamic_index_in_dim(w_got, 1 - core, 1, keepdims=False).reshape(tm * shard, width)
    w_recv = exchange(w_send)
    w_block = jnp.concatenate(
        [jnp.where(first, w_keep, w_recv), jnp.where(first, w_recv, w_keep)], axis=0
    )
    block = w_block.shape[0]

    sent = jnp.concatenate([by_patch(frames_in), by_patch(out_grad)], axis=1)
    sent, w_block = lax.optimization_barrier((sent, w_block))
    got = swap(sent.reshape(-1, width), TM).reshape(tm, 2 * per_peer, width)

    pieces = []
    for part in (w_block, across_x(w_block)):
        pieces += [part] + [along_y(part, step) for step in range(1, Y_SIZE)]
    got_other = exchange(got)

    shape = jax.ShapeDtypeStruct
    token = pl.pallas_call(
        arrived_kernel,
        in_specs=[ANY] * 8,
        out_specs=VMEM,
        out_shape=shape((8, 128), f32),
        compiler_params=vmem_params(),
        cost_estimate=pl.CostEstimate(flops=2 * 10**10, bytes_accessed=4 * 2**20, transcendentals=0),
        name="arrived",
    )(*pieces)

    sample_shapes = (shape((rows, HALF), bf16), shape((rows, width), f32))
    half_shape, own_shape = shape((block, width), bf16), shape((block, width), f32)
    w_mine, mixed, d_normed, mixed_2, d_normed_2, *grad_pieces = pl.pallas_call(
        functools.partial(layer_kernel, patches),
        in_specs=[ANY, ANY, VMEM, VMEM] + [ANY] * 8,
        out_specs=(ANY,) * 13,
        out_shape=(shape((width, HALF), bf16),)
        + sample_shapes * 2 + ((own_shape,) + (half_shape,) * (Y_SIZE - 1)) * 2,
        scratch_shapes=[
            pltpu.VMEM((2,) + got.shape, bf16),
            pltpu.VMEM((width, width), bf16),
            pltpu.VMEM((2, rows, width), bf16),
            pltpu.VMEM((2, rows, HALF), bf16),
            pltpu.VMEM((2, rows, 3 * HALF), bf16),
            pltpu.VMEM((2, rows, width), f32),
            pltpu.VMEM((2 * block, width), f32),
            pltpu.VMEM((2, block, width), f32),
            pltpu.VMEM((6, block, width), bf16),
            pltpu.VMEM((HALF // DH, rows, rows), f32),
            pltpu.VMEM((HALF // DH, rows, rows), f32),
            pltpu.VMEM((HALF // DH, rows, rows), bf16),
            pltpu.VMEM((HALF // DH, rows, rows), bf16),
            pltpu.SemaphoreType.DMA((10,)),
            pltpu.SemaphoreType.DMA((13,)),
        ],
        compiler_params=vmem_params(60),
        cost_estimate=pl.CostEstimate(flops=3 * 10**10, bytes_accessed=10 * 2**20, transcendentals=2**19),
        name="layer",
    )(got, got_other, gain_row, token, *pieces)
    w_other = exchange(w_mine)
    d_normed_other = exchange(d_normed_2)
    mixed_other = exchange(mixed_2)

    received = [along_y(grad_pieces[Y_SIZE + step], step) for step in range(1, Y_SIZE)]
    partial = grad_pieces[Y_SIZE] + sum(piece.astype(f32) for piece in received)
    received = [along_y(grad_pieces[step], step) for step in range(1, Y_SIZE)]
    grads = pl.pallas_call(
        sum_kernel,
        in_specs=[VMEM] * 5,
        out_shape=shape((tm, 2 * shard, width), bf16),
        compiler_params=vmem_params(8),
        cost_estimate=pl.CostEstimate(flops=10**10, bytes_accessed=2 * 2**20, transcendentals=0),
        name="sum_blocks",
    )(grad_pieces[0], *received, across_x(partial.astype(bf16)))

    sent = pl.pallas_call(
        input_kernel,
        out_shape=shape((tm, 3 * per_peer, width // 2), bf16),
        in_specs=[ANY] * 3 + [VMEM] * 3,
        out_specs=ANY,
        scratch_shapes=[
            pltpu.VMEM(got.shape, bf16),
            pltpu.VMEM((rows, width), f32),
            pltpu.VMEM((rows, HALF), bf16),
            pltpu.VMEM((tm, 3 * per_peer, width // 2), bf16),
            pltpu.SemaphoreType.DMA((11,)),
        ],
        compiler_params=vmem_params(24),
        cost_estimate=pl.CostEstimate(flops=10**9, bytes_accessed=6 * 2**20, transcendentals=0),
        name="input_gradient",
    )(got, d_normed, mixed, d_normed_other, mixed_other, gain_row)
    got = swap(sent.reshape(-1, width // 2), TM).reshape(sent.shape)
    grads, got = lax.optimization_barrier((grads, got))
    local = shape(frames_in.shape[1:], bf16)
    result, grad_in = pl.pallas_call(
        home_kernel,
        in_specs=[ANY] * 4,
        out_specs=(ANY,) * 2,
        out_shape=(local,) * 2,
        scratch_shapes=[
            pltpu.VMEM(sent.shape, bf16),
            pltpu.VMEM(local.shape, bf16),
            pltpu.VMEM((width, HALF), bf16),
            pltpu.VMEM((width, HALF), bf16),
            pltpu.VMEM(local.shape, bf16),
            pltpu.VMEM(local.shape, bf16),
            pltpu.SemaphoreType.DMA((4,)),
        ],
        compiler_params=vmem_params(),
        cost_estimate=pl.CostEstimate(flops=3 * 10**8, bytes_accessed=4 * 2**20, transcendentals=0),
        name="home",
    )(got, frames_in[0], w_mine, w_other)

    grads = swap(grads.reshape(-1, width), TM)
    grads, result, grad_in = lax.optimization_barrier((grads, result, grad_in))
    total = jnp.sum(grads.reshape(tm, 2, shard, width).astype(f32), axis=0)
    keep = lax.dynamic_index_in_dim(total, core, 0, keepdims=False)
    recv = exchange(lax.dynamic_index_in_dim(total, 1 - core, 0, keepdims=False))
    low = jnp.where(first, keep, recv).reshape(shard, 4, 1, HALF)
    high = jnp.where(first, recv, keep).reshape(shard, 4, 1, HALF)
    whole = jnp.concatenate([low, high], axis=2)
    grad_qkv = whole[:, :3].reshape(shard, 6 * HALF)
    grad_out = whole[:, 3].reshape(shard, 2 * HALF).T
    own_row = lax.axis_index(DP + TM) * shard
    grad_gain = jnp.sum(w_qkv.astype(f32) * grad_qkv, axis=1) / lax.dynamic_slice_in_dim(gain, own_row, shard)
    return (result[None], grad_in[None], grad_qkv, grad_out, grad_gain)


def solution(mesh):
    fine = Mesh(mesh.devices.reshape(Y_SIZE, XH_SIZE, 2, 2, 8), DP + TM)
    in_specs = (
        P(DP, TM, None, None),
        P(),
        P(DP + TM, None),
        P(None, DP + TM),
        P(DP, TM, None, None),
    )
    out_specs = (
        P(DP, TM, None, None),
        P(DP, TM, None, None),
        P(DP + TM, None),
        P(None, DP + TM),
        P(DP + TM),
    )
    return jax.shard_map(body, mesh=fine, in_specs=in_specs, out_specs=out_specs, check_vma=False)
```

```python
import functools

import jax
import jax.numpy as jnp
from jax import lax
from jax.experimental import pallas as pl
from jax.experimental.pallas import tpu as pltpu
from jax.sharding import Mesh, PartitionSpec as P

DP = ("y", "xh", "core")
TM = ("xl", "z")
Y_SIZE, XH_SIZE, TM_SIZE = 4, 2, 16

D = 1024
DH = 64
HALF = 256
norm_eps = 1e-05
f32 = jnp.float32
bf16 = jnp.bfloat16

NN = (((1,), (0,)), ((), ()))
NT = (((1,), (1,)), ((), ()))
TN = (((0,), (0,)), ((), ()))

VMEM = pl.BlockSpec(memory_space=pltpu.VMEM)
ANY = pl.BlockSpec(memory_space=pl.ANY)


def mm(a, b, dims):
    return lax.dot_general(a, b, dims, preferred_element_type=f32)


def layer_stats(features):
    wide = features.astype(f32)
    centred = wide - jnp.mean(wide, axis=-1, keepdims=True)
    inv_std = lax.rsqrt(jnp.mean(centred * centred, axis=-1, keepdims=True) + norm_eps)
    return centred * inv_std, inv_std


def pack_weights_kernel(w_qkv_ref, w_out_ref, out_ref):
    qkv, out = w_qkv_ref[...].astype(f32), w_out_ref[...].astype(f32)
    halves = []
    for half in range(2):
        parts = [qkv[:, (2 * part + half) * HALF : (2 * part + half + 1) * HALF] for part in range(3)]
        halves.append(jnp.concatenate(parts + [out[:, half * HALF : (half + 1) * HALF]], axis=1))
    both = jnp.concatenate(halves, axis=0)
    out_ref[...] = jnp.broadcast_to(both[None], out_ref.shape).astype(bf16)


def fetch(pairs, sems, first=0):
    copies = [pltpu.make_async_copy(src, dst, sems.at[first + i]) for i, (src, dst) in enumerate(pairs)]
    for copy in copies:
        copy.start()
    return copies


def wait_all(copies):
    for copy in copies:
        copy.wait()


CHUNK = 64


def sample(patches, got, gain_ref, weights, normed, mixed, dpacked, slots, before_weights):
    scores, d_probs, low_probs, d_scores = slots
    rows = normed.shape[0]
    per_peer = got.shape[1] // 2
    group = 4
    for peer in range(0, got.shape[0], group):
        features = got[peer : peer + group, :per_peer, :].reshape(group * per_peer, D)
        normal_x, _ = layer_stats(features)
        normed[peer * per_peer : (peer + group) * per_peer, :] = (normal_x * gain_ref[...]).astype(bf16)
    before_weights()
    packed = mm(normed[...], weights[:, : 3 * HALF], NN).astype(bf16)
    d_mixed = mm(got[:, per_peer:, :].reshape(rows, D), weights[:, 3 * HALF :], NN).astype(bf16)
    row_patch = lax.broadcasted_iota(jnp.int32, (CHUNK, rows), 0) % patches
    col_patch = lax.broadcasted_iota(jnp.int32, (CHUNK, rows), 1) % patches
    bias = jnp.where(row_patch == col_patch, 0.0, -1e30)
    low_half = lax.broadcasted_iota(jnp.int32, (rows, 2 * DH), 1) < DH
    zero = jnp.zeros((rows, 2 * DH), bf16)
    heads = HALF // DH

    def part(index, head):
        lo = index * HALF + head // 2 * 2 * DH
        return packed[:, lo : lo + 2 * DH]

    def d_part(head):
        lo = head // 2 * 2 * DH
        return d_mixed[:, lo : lo + 2 * DH]

    for head in range(heads):
        own = low_half if head % 2 == 0 else jnp.logical_not(low_half)
        query = jnp.where(own, part(0, head) * DH ** (-0.5), zero)
        scores[head] = mm(query, part(1, head), NT)
        d_probs[head] = mm(jnp.where(own, d_part(head), zero), part(2, head), NT)
    for pair in range(heads // 2):
        outs = []
        for head in (2 * pair, 2 * pair + 1):
            for at in range(0, rows, CHUNK):
                score = scores[head, at : at + CHUNK, :] + bias
                expo = jnp.exp(score - jnp.max(score, axis=-1, keepdims=True))
                prob = expo * (1.0 / jnp.sum(expo, axis=-1, keepdims=True))
                low_probs[head, at : at + CHUNK, :] = prob.astype(bf16)
                d_prob = d_probs[head, at : at + CHUNK, :]
                inner = jnp.sum(d_prob * prob, axis=-1, keepdims=True)
                d_scores[head, at : at + CHUNK, :] = (prob * (d_prob - inner)).astype(bf16)
            outs.append(
                (
                    mm(low_probs[head], part(2, head), NN),
                    mm(d_scores[head], part(1, head), NN) * DH ** (-0.5),
                    mm(d_scores[head], part(0, head), TN) * DH ** (-0.5),
                    mm(low_probs[head], d_part(head), TN),
                )
            )
        outs = [jnp.where(low_half, low, high).astype(bf16) for low, high in zip(*outs)]
        lo = pair * 2 * DH
        mixed[:, lo : lo + 2 * DH] = outs[0]
        for index in range(3):
            at = index * HALF + lo
            dpacked[:, at : at + 2 * DH] = outs[1 + index]


def block_of(step, side):
    y, xh = lax.axis_index("y"), lax.axis_index("xh")
    return lax.rem(y + step + Y_SIZE, Y_SIZE) * XH_SIZE + lax.rem(xh + side, XH_SIZE)


def arrived_kernel(*refs):
    refs[-1][...] = jnp.zeros_like(refs[-1])


def layer_kernel(patches, got_own_ref, got_other_ref, gain_ref, token_ref, *refs):
    pieces, outs, grad_refs, scratch = refs[:8], refs[8:11], refs[11:19], refs[19:]
    w_ref, for_own_ref, for_other_ref = outs
    got, weights, normed, mixed, dpacked, for_own, for_other, grads, own, peers = scratch[:10]
    slots, (sems, out_sems) = scratch[10:14], scratch[14:]
    copies = fetch([(got_own_ref, got.at[0])], sems)
    block = own.shape[1]
    places = [block_of(-(i % Y_SIZE), i // Y_SIZE) for i in range(8)]
    starts = [pl.multiple_of(place * block, block) for place in places]
    copies += fetch([(p, weights.at[pl.ds(at, block), :]) for p, at in zip(pieces, starts)], sems, 1)
    copies += fetch([(got_other_ref, got.at[1])], sems, 9)
    results = []
    per_peer = got.shape[2] // 2

    def before_weights():
        wait_all(copies[1:9])
        results.extend(fetch([(weights.at[:, 3 * HALF :], w_ref)], out_sems))

    copies[0].wait()
    arguments = (got.at[0], gain_ref, weights, normed.at[0], mixed.at[0], dpacked.at[0])
    sample(patches, *arguments, slots, before_weights)
    for_own[:, :D] = mm(dpacked[0], weights[:, : 3 * HALF], NT)
    for_own[:, D:] = mixed[0].astype(f32)
    results += fetch([(for_own, for_own_ref)], out_sems, 1)
    copies[9].wait()
    arguments = (got.at[1], gain_ref, weights, normed.at[1], mixed.at[1], dpacked.at[1])
    sample(patches, *arguments, slots, lambda: None)
    for_other[:, :D] = mm(dpacked[1], weights[:, : 3 * HALF], NT).astype(bf16)
    for_other[:, D:] = mixed[1]
    results += fetch([(for_other, for_other_ref)], out_sems, 2)
    rows = normed.shape[1]
    pair_rows = 2 * block
    all_dpacked = dpacked[...].reshape(2 * rows, 3 * HALF)
    all_mixed = mixed[...].reshape(2 * rows, HALF)
    y, xh = lax.axis_index("y"), lax.axis_index("xh")
    for step in (1, 2, 3, 0):
        start = pl.multiple_of(lax.rem(y + step, Y_SIZE) * pair_rows, pair_rows)
        columns = pl.ds(start, pair_rows)
        grads[:, : 3 * HALF] = mm(normed[:, :, columns].reshape(2 * rows, pair_rows), all_dpacked, TN)
        grads[:, 3 * HALF :] = mm(got[:, :, per_peer:, columns].reshape(2 * rows, pair_rows), all_mixed, TN)
        for side in range(XH_SIZE):
            start = pl.multiple_of(lax.rem(xh + side, XH_SIZE) * block, block)
            slot = own.at[side] if step == 0 else peers.at[side * (Y_SIZE - 1) + step - 1]
            slot[...] = grads[pl.ds(start, block), :].astype(slot.dtype)
            results += fetch([(slot, grad_refs[side * Y_SIZE + step])], out_sems, len(results))
    wait_all(results)


def input_kernel(got_ref, mine_ref, other, gain_ref, out_ref, got, mine, out, sems):
    copies = fetch([(got_ref, got), (mine_ref, mine)], sems)
    peers, per_peer = got.shape[0], got.shape[1] // 2
    wait_all(copies)
    results = []
    group = 4
    half = (group, per_peer, D // 2)
    for peer in range(0, peers, group):
        at = slice(peer, peer + group)
        rows = slice(peer * per_peer, (peer + group) * per_peer)
        normal_x, inv_std = layer_stats(got[at, :per_peer, :].reshape(group * per_peer, D))
        scaled = (mine[rows, :D] + other[rows, :D].astype(f32)).astype(bf16).astype(f32) * gain_ref[...]
        d_input = inv_std * (
            scaled
            - jnp.mean(scaled, axis=-1, keepdims=True)
            - normal_x * jnp.mean(scaled * normal_x, axis=-1, keepdims=True)
        )
        grad_in = (got[at, per_peer:, :].reshape(group * per_peer, D).astype(f32) + d_input).astype(bf16)
        out[at, :per_peer, :] = grad_in[:, : D // 2].reshape(half)
        out[at, per_peer : 2 * per_peer, :] = grad_in[:, D // 2 :].reshape(half)
        out[at, 2 * per_peer :, :HALF] = mine[rows, D:].astype(bf16).reshape(group, per_peer, HALF)
        out[at, 2 * per_peer :, HALF:] = other[rows, D:].reshape(group, per_peer, HALF)
        results += fetch([(out.at[at], out_ref.at[at])], sems, 2 + len(results))
    wait_all(results)


def sum_kernel(own_ref, a_ref, b_ref, c_ref, across_ref, out_ref):
    total = own_ref[...] + a_ref[...].astype(f32) + b_ref[...].astype(f32) + c_ref[...].astype(f32)
    total = total + across_ref[...].astype(f32)
    shard = 4
    low, high = (total.reshape(2, -1, 2 * shard, D)[core] for core in range(2))
    top = lax.broadcasted_iota(jnp.int32, low.shape, 1) < shard
    even = jnp.where(top, low, pltpu.roll(high, shard, 1))
    odd = jnp.where(top, pltpu.roll(low, shard, 1), high)
    out_ref[...] = jnp.stack([even, odd], axis=1).reshape(out_ref.shape).astype(bf16)


def home_kernel(got_ref, x_ref, w_mine_ref, w_other_ref, result_ref, grad_ref, got, x, w_mine, w_other, result, grad, sems):
    wait_all(
        fetch(
            [(got_ref, got), (x_ref, x), (w_mine_ref, w_mine), (w_other_ref, w_other)],
            sems,
        )
    )
    peers, _, width = got.shape
    frames, count, _ = x.shape
    patches = count // peers
    per_peer = frames * patches

    def by_frame(part):
        wide = got[:, part * per_peer : (part + 1) * per_peer, :].astype(f32)
        wide = wide.reshape(peers, frames, patches, width)
        return [wide[:, f].reshape(count, width).astype(bf16) for f in range(frames)]

    low, high, heads = by_frame(0), by_frame(1), by_frame(2)
    for f in range(frames):
        grad[f, :, :width] = low[f]
        grad[f, :, width:] = high[f]
    results = fetch([(grad, grad_ref)], sems)
    for f in range(frames):
        projected = mm(heads[f][:, :HALF], w_mine[...], NT) + mm(heads[f][:, HALF:], w_other[...], NT)
        result[f] = (x[f].astype(f32) + projected).astype(bf16)
    wait_all(results + fetch([(result, result_ref)], sems, 1))


def vmem_params(mib=60):
    return pltpu.CompilerParams(vmem_limit_bytes=mib * 2**20)


def exchange(value):
    return lax.ppermute(value, "core", [(0, 1), (1, 0)])


def swap(value, axes):
    return lax.all_to_all(value, axes, split_axis=0, concat_axis=0, tiled=True)


def along_y(value, step):
    return lax.ppermute(value, "y", [(i, (i + step) % Y_SIZE) for i in range(Y_SIZE)])


def across_x(value):
    return lax.ppermute(value, "xh", [(0, 1), (1, 0)])


def body(frames_in, gain, w_qkv, w_out, out_grad):
    _, frames, patch_count, width = frames_in.shape
    tm = TM_SIZE
    patches = patch_count // tm
    per_peer = frames * patches
    rows = tm * per_peer
    shard = w_qkv.shape[0]
    core = lax.axis_index("core")
    first = core == 0
    gain_row = gain.reshape(1, width)

    def by_patch(value):
        value = value.reshape(frames, tm, patches, width).transpose(1, 0, 2, 3)
        return value.reshape(tm, per_peer, width)

    w_parts = pl.pallas_call(
        pack_weights_kernel,
        out_shape=jax.ShapeDtypeStruct((tm, 2 * shard, width), bf16),
        in_specs=[VMEM] * 2,
        compiler_params=vmem_params(),
        cost_estimate=pl.CostEstimate(flops=0, bytes_accessed=2**18, transcendentals=0),
        name="pack_weights",
    )(w_qkv, w_out.T)
    w_got = swap(w_parts.reshape(-1, width), TM).reshape(tm, 2, shard, width)

    w_keep = lax.dynamic_index_in_dim(w_got, core, 1, keepdims=False).reshape(tm * shard, width)
    w_send = lax.dynamic_index_in_dim(w_got, 1 - core, 1, keepdims=False).reshape(tm * shard, width)
    w_recv = exchange(w_send)
    w_block = jnp.concatenate(
        [jnp.where(first, w_keep, w_recv), jnp.where(first, w_recv, w_keep)], axis=0
    )
    block = w_block.shape[0]

    sent = jnp.concatenate([by_patch(frames_in), by_patch(out_grad)], axis=1)
    sent, w_block = lax.optimization_barrier((sent, w_block))
    got = swap(sent.reshape(-1, width), TM).reshape(tm, 2 * per_peer, width)

    pieces = []
    for part in (w_block, across_x(w_block)):
        pieces += [part] + [along_y(part, step) for step in range(1, Y_SIZE)]
    got_other = exchange(got)

    shape = jax.ShapeDtypeStruct
    token = pl.pallas_call(
        arrived_kernel,
        in_specs=[ANY] * 8,
        out_specs=VMEM,
        out_shape=shape((8, 128), f32),
        compiler_params=vmem_params(),
        cost_estimate=pl.CostEstimate(flops=2 * 10**10, bytes_accessed=4 * 2**20, transcendentals=0),
        name="arrived",
    )(*pieces)

    sample_shapes = (shape((rows, width + HALF), f32), shape((rows, width + HALF), bf16))
    half_shape, own_shape = shape((block, width), bf16), shape((block, width), f32)
    w_mine, for_own, for_other, *grad_pieces = pl.pallas_call(
        functools.partial(layer_kernel, patches),
        in_specs=[ANY, ANY, VMEM, VMEM] + [ANY] * 8,
        out_specs=(ANY,) * 11,
        out_shape=(shape((width, HALF), bf16),)
        + sample_shapes + ((own_shape,) + (half_shape,) * (Y_SIZE - 1)) * 2,
        scratch_shapes=[
            pltpu.VMEM((2,) + got.shape, bf16),
            pltpu.VMEM((width, width), bf16),
            pltpu.VMEM((2, rows, width), bf16),
            pltpu.VMEM((2, rows, HALF), bf16),
            pltpu.VMEM((2, rows, 3 * HALF), bf16),
            pltpu.VMEM((rows, width + HALF), f32),
            pltpu.VMEM((rows, width + HALF), bf16),
            pltpu.VMEM((2 * block, width), f32),
            pltpu.VMEM((2, block, width), f32),
            pltpu.VMEM((6, block, width), bf16),
            pltpu.VMEM((HALF // DH, rows, rows), f32),
            pltpu.VMEM((HALF // DH, rows, rows), f32),
            pltpu.VMEM((HALF // DH, rows, rows), bf16),
            pltpu.VMEM((HALF // DH, rows, rows), bf16),
            pltpu.SemaphoreType.DMA((10,)),
            pltpu.SemaphoreType.DMA((11,)),
        ],
        compiler_params=vmem_params(60),
        cost_estimate=pl.CostEstimate(flops=3 * 10**10, bytes_accessed=10 * 2**20, transcendentals=2**19),
        name="layer",
    )(got, got_other, gain_row, token, *pieces)
    w_other = exchange(w_mine)
    from_other = exchange(for_other)

    received = [along_y(grad_pieces[Y_SIZE + step], step) for step in range(1, Y_SIZE)]
    partial = grad_pieces[Y_SIZE] + sum(piece.astype(f32) for piece in received)
    received = [along_y(grad_pieces[step], step) for step in range(1, Y_SIZE)]
    grads = pl.pallas_call(
        sum_kernel,
        in_specs=[VMEM] * 5,
        out_shape=shape((tm, 2 * shard, width), bf16),
        compiler_params=vmem_params(8),
        cost_estimate=pl.CostEstimate(flops=10**10, bytes_accessed=2 * 2**20, transcendentals=0),
        name="sum_blocks",
    )(grad_pieces[0], *received, across_x(partial.astype(bf16)))

    sent = pl.pallas_call(
        input_kernel,
        out_shape=shape((tm, 3 * per_peer, width // 2), bf16),
        in_specs=[ANY] * 2 + [VMEM] * 2,
        out_specs=ANY,
        scratch_shapes=[
            pltpu.VMEM(got.shape, bf16),
            pltpu.VMEM((rows, width + HALF), f32),
            pltpu.VMEM((tm, 3 * per_peer, width // 2), bf16),
            pltpu.SemaphoreType.DMA((6,)),
        ],
        compiler_params=vmem_params(24),
        cost_estimate=pl.CostEstimate(flops=10**9, bytes_accessed=6 * 2**20, transcendentals=0),
        name="input_gradient",
    )(got, for_own, from_other, gain_row)
    got = swap(sent.reshape(-1, width // 2), TM).reshape(sent.shape)
    grads, got = lax.optimization_barrier((grads, got))
    local = shape(frames_in.shape[1:], bf16)
    result, grad_in = pl.pallas_call(
        home_kernel,
        in_specs=[ANY] * 4,
        out_specs=(ANY,) * 2,
        out_shape=(local,) * 2,
        scratch_shapes=[
            pltpu.VMEM(sent.shape, bf16),
            pltpu.VMEM(local.shape, bf16),
            pltpu.VMEM((width, HALF), bf16),
            pltpu.VMEM((width, HALF), bf16),
            pltpu.VMEM(local.shape, bf16),
            pltpu.VMEM(local.shape, bf16),
            pltpu.SemaphoreType.DMA((4,)),
        ],
        compiler_params=vmem_params(),
        cost_estimate=pl.CostEstimate(flops=3 * 10**8, bytes_accessed=4 * 2**20, transcendentals=0),
        name="home",
    )(got, frames_in[0], w_mine, w_other)

    grads = swap(grads.reshape(-1, width), TM)
    grads, result, grad_in = lax.optimization_barrier((grads, result, grad_in))
    total = jnp.sum(grads.reshape(tm, 2, shard, width).astype(f32), axis=0)
    keep = lax.dynamic_index_in_dim(total, core, 0, keepdims=False)
    recv = exchange(lax.dynamic_index_in_dim(total, 1 - core, 0, keepdims=False))
    low = jnp.where(first, keep, recv).reshape(shard, 4, 1, HALF)
    high = jnp.where(first, recv, keep).reshape(shard, 4, 1, HALF)
    whole = jnp.concatenate([low, high], axis=2)
    grad_qkv = whole[:, :3].reshape(shard, 6 * HALF)
    grad_out = whole[:, 3].reshape(shard, 2 * HALF).T
    own_row = lax.axis_index(DP + TM) * shard
    grad_gain = jnp.sum(w_qkv.astype(f32) * grad_qkv, axis=1) / lax.dynamic_slice_in_dim(gain, own_row, shard)
    return (result[None], grad_in[None], grad_qkv, grad_out, grad_gain)


def solution(mesh):
    fine = Mesh(mesh.devices.reshape(Y_SIZE, XH_SIZE, 2, 2, 8), DP + TM)
    in_specs = (
        P(DP, TM, None, None),
        P(),
        P(DP + TM, None),
        P(None, DP + TM),
        P(DP, TM, None, None),
    )
    out_specs = (
        P(DP, TM, None, None),
        P(DP, TM, None, None),
        P(DP + TM, None),
        P(None, DP + TM),
        P(DP + TM),
    )
    return jax.shard_map(body, mesh=fine, in_specs=in_specs, out_specs=out_specs, check_vma=False)
```

```python
import functools

import jax
import jax.numpy as jnp
from jax import lax
from jax.experimental import pallas as pl
from jax.experimental.pallas import tpu as pltpu
from jax.sharding import Mesh, PartitionSpec as P

DP = ("y", "xh", "core")
TM = ("xl", "z")
Y_SIZE, XH_SIZE, TM_SIZE = 4, 2, 16

D = 1024
DH = 64
HALF = 256
norm_eps = 1e-05
f32 = jnp.float32
bf16 = jnp.bfloat16

NN = (((1,), (0,)), ((), ()))
NT = (((1,), (1,)), ((), ()))
TN = (((0,), (0,)), ((), ()))

VMEM = pl.BlockSpec(memory_space=pltpu.VMEM)
ANY = pl.BlockSpec(memory_space=pl.ANY)


def mm(a, b, dims):
    return lax.dot_general(a, b, dims, preferred_element_type=f32)


def layer_stats(features):
    wide = features.astype(f32)
    centred = wide - jnp.mean(wide, axis=-1, keepdims=True)
    inv_std = lax.rsqrt(jnp.mean(centred * centred, axis=-1, keepdims=True) + norm_eps)
    return centred * inv_std, inv_std


def pack_weights_kernel(w_qkv_ref, w_out_ref, out_ref):
    qkv, out = w_qkv_ref[...].astype(f32), w_out_ref[...].astype(f32)
    halves = []
    for half in range(2):
        parts = [qkv[:, (2 * part + half) * HALF : (2 * part + half + 1) * HALF] for part in range(3)]
        halves.append(jnp.concatenate(parts + [out[:, half * HALF : (half + 1) * HALF]], axis=1))
    both = jnp.concatenate(halves, axis=0)
    out_ref[...] = jnp.broadcast_to(both[None], out_ref.shape).astype(bf16)


def fetch(pairs, sems, first=0):
    copies = [pltpu.make_async_copy(src, dst, sems.at[first + i]) for i, (src, dst) in enumerate(pairs)]
    for copy in copies:
        copy.start()
    return copies


def wait_all(copies):
    for copy in copies:
        copy.wait()


CHUNK = 64


def sample(patches, got, gain_ref, weights, normed, mixed, dpacked, slots, before_weights):
    scores, d_probs, low_probs, d_scores = slots
    rows = normed.shape[0]
    per_peer = got.shape[1] // 2
    group = 4
    for peer in range(0, got.shape[0], group):
        features = got[peer : peer + group, :per_peer, :].reshape(group * per_peer, D)
        normal_x, _ = layer_stats(features)
        normed[peer * per_peer : (peer + group) * per_peer, :] = (normal_x * gain_ref[...]).astype(bf16)
    before_weights()
    packed = mm(normed[...], weights[:, : 3 * HALF], NN).astype(bf16)
    d_mixed = mm(got[:, per_peer:, :].reshape(rows, D), weights[:, 3 * HALF :], NN).astype(bf16)
    row_patch = lax.broadcasted_iota(jnp.int32, (CHUNK, rows), 0) % patches
    col_patch = lax.broadcasted_iota(jnp.int32, (CHUNK, rows), 1) % patches
    bias = jnp.where(row_patch == col_patch, 0.0, -1e30)
    low_half = lax.broadcasted_iota(jnp.int32, (rows, 2 * DH), 1) < DH
    zero = jnp.zeros((rows, 2 * DH), bf16)
    heads = HALF // DH

    def part(index, head):
        lo = index * HALF + head // 2 * 2 * DH
        return packed[:, lo : lo + 2 * DH]

    def d_part(head):
        lo = head // 2 * 2 * DH
        return d_mixed[:, lo : lo + 2 * DH]

    for head in range(heads):
        own = low_half if head % 2 == 0 else jnp.logical_not(low_half)
        query = jnp.where(own, part(0, head) * DH ** (-0.5), zero)
        scores[head] = mm(query, part(1, head), NT)
        d_probs[head] = mm(jnp.where(own, d_part(head), zero), part(2, head), NT)
    for pair in range(heads // 2):
        outs = []
        for head in (2 * pair, 2 * pair + 1):
            for at in range(0, rows, CHUNK):
                score = scores[head, at : at + CHUNK, :] + bias
                expo = jnp.exp(score - jnp.max(score, axis=-1, keepdims=True))
                prob = expo * (1.0 / jnp.sum(expo, axis=-1, keepdims=True))
                low_probs[head, at : at + CHUNK, :] = prob.astype(bf16)
                d_prob = d_probs[head, at : at + CHUNK, :]
                inner = jnp.sum(d_prob * prob, axis=-1, keepdims=True)
                d_scores[head, at : at + CHUNK, :] = (prob * (d_prob - inner)).astype(bf16)
            outs.append(
                (
                    mm(low_probs[head], part(2, head), NN),
                    mm(d_scores[head], part(1, head), NN) * DH ** (-0.5),
                    mm(d_scores[head], part(0, head), TN) * DH ** (-0.5),
                    mm(low_probs[head], d_part(head), TN),
                )
            )
        outs = [jnp.where(low_half, low, high).astype(bf16) for low, high in zip(*outs)]
        lo = pair * 2 * DH
        mixed[:, lo : lo + 2 * DH] = outs[0]
        for index in range(3):
            at = index * HALF + lo
            dpacked[:, at : at + 2 * DH] = outs[1 + index]


def block_of(step, side):
    y, xh = lax.axis_index("y"), lax.axis_index("xh")
    return lax.rem(y + step + Y_SIZE, Y_SIZE) * XH_SIZE + lax.rem(xh + side, XH_SIZE)


def arrived_kernel(*refs):
    refs[-1][...] = jnp.zeros_like(refs[-1])


def layer_kernel(patches, got_own_ref, got_other_ref, gain_ref, token_ref, *refs):
    pieces, outs, grad_refs, scratch = refs[:8], refs[8:11], refs[11:19], refs[19:]
    w_ref, for_own_ref, for_other_ref = outs
    got, weights, normed, mixed, dpacked, for_own, for_other, grads, own, peers = scratch[:10]
    slots, (sems, out_sems) = scratch[10:14], scratch[14:]
    copies = fetch([(got_own_ref, got.at[0])], sems)
    block = own.shape[1]
    places = [block_of(-(i % Y_SIZE), i // Y_SIZE) for i in range(8)]
    starts = [pl.multiple_of(place * block, block) for place in places]
    copies += fetch([(p, weights.at[pl.ds(at, block), :]) for p, at in zip(pieces, starts)], sems, 1)
    copies += fetch([(got_other_ref, got.at[1])], sems, 9)
    results = []
    per_peer = got.shape[2] // 2

    def before_weights():
        wait_all(copies[1:9])
        results.extend(fetch([(weights.at[:, 3 * HALF :], w_ref)], out_sems))

    copies[0].wait()
    arguments = (got.at[0], gain_ref, weights, normed.at[0], mixed.at[0], dpacked.at[0])
    sample(patches, *arguments, slots, before_weights)
    for_own[:, :D] = mm(dpacked[0], weights[:, : 3 * HALF], NT)
    for_own[:, D:] = mixed[0].astype(f32)
    results += fetch([(for_own, for_own_ref)], out_sems, 1)
    copies[9].wait()
    arguments = (got.at[1], gain_ref, weights, normed.at[1], mixed.at[1], dpacked.at[1])
    sample(patches, *arguments, slots, lambda: None)
    for_other[:, :D] = mm(dpacked[1], weights[:, : 3 * HALF], NT).astype(bf16)
    for_other[:, D:] = mixed[1]
    results += fetch([(for_other, for_other_ref)], out_sems, 2)
    rows = normed.shape[1]
    pair_rows = 2 * block
    all_dpacked = dpacked[...].reshape(2 * rows, 3 * HALF)
    all_mixed = mixed[...].reshape(2 * rows, HALF)
    for part in range(Y_SIZE):
        columns = slice(part * pair_rows, (part + 1) * pair_rows)
        grads[columns, : 3 * HALF] = mm(normed[:, :, columns].reshape(2 * rows, pair_rows), all_dpacked, TN)
        grads[columns, 3 * HALF :] = mm(got[:, :, per_peer:, columns].reshape(2 * rows, pair_rows), all_mixed, TN)
    for step in (1, 2, 3, 0):
        for side in range(XH_SIZE):
            start = pl.multiple_of(block_of(step, side) * block, block)
            slot = own.at[side] if step == 0 else peers.at[side * (Y_SIZE - 1) + step - 1]
            slot[...] = grads[pl.ds(start, block), :].astype(slot.dtype)
            results += fetch([(slot, grad_refs[side * Y_SIZE + step])], out_sems, len(results))
    wait_all(results)


def input_kernel(got_ref, mine_ref, other, gain_ref, out_ref, got, mine, out, sems):
    copies = fetch([(got_ref, got), (mine_ref, mine)], sems)
    peers, per_peer = got.shape[0], got.shape[1] // 2
    wait_all(copies)
    results = []
    group = 4
    half = (group, per_peer, D // 2)
    for peer in range(0, peers, group):
        at = slice(peer, peer + group)
        rows = slice(peer * per_peer, (peer + group) * per_peer)
        normal_x, inv_std = layer_stats(got[at, :per_peer, :].reshape(group * per_peer, D))
        scaled = (mine[rows, :D] + other[rows, :D].astype(f32)).astype(bf16).astype(f32) * gain_ref[...]
        d_input = inv_std * (
            scaled
            - jnp.mean(scaled, axis=-1, keepdims=True)
            - normal_x * jnp.mean(scaled * normal_x, axis=-1, keepdims=True)
        )
        grad_in = (got[at, per_peer:, :].reshape(group * per_peer, D).astype(f32) + d_input).astype(bf16)
        out[at, :per_peer, :] = grad_in[:, : D // 2].reshape(half)
        out[at, per_peer : 2 * per_peer, :] = grad_in[:, D // 2 :].reshape(half)
        out[at, 2 * per_peer :, :HALF] = mine[rows, D:].astype(bf16).reshape(group, per_peer, HALF)
        out[at, 2 * per_peer :, HALF:] = other[rows, D:].reshape(group, per_peer, HALF)
        results += fetch([(out.at[at], out_ref.at[at])], sems, 2 + len(results))
    wait_all(results)


def sum_kernel(own_ref, a_ref, b_ref, c_ref, across_ref, out_ref):
    total = own_ref[...] + a_ref[...].astype(f32) + b_ref[...].astype(f32) + c_ref[...].astype(f32)
    total = total + across_ref[...].astype(f32)
    shard = 4
    low, high = (total.reshape(2, -1, 2 * shard, D)[core] for core in range(2))
    top = lax.broadcasted_iota(jnp.int32, low.shape, 1) < shard
    even = jnp.where(top, low, pltpu.roll(high, shard, 1))
    odd = jnp.where(top, pltpu.roll(low, shard, 1), high)
    out_ref[...] = jnp.stack([even, odd], axis=1).reshape(out_ref.shape).astype(bf16)


def home_kernel(got_ref, x_ref, w_mine_ref, w_other_ref, result_ref, grad_ref, got, x, w_mine, w_other, result, grad, sems):
    wait_all(
        fetch(
            [(got_ref, got), (x_ref, x), (w_mine_ref, w_mine), (w_other_ref, w_other)],
            sems,
        )
    )
    peers, _, width = got.shape
    frames, count, _ = x.shape
    patches = count // peers
    per_peer = frames * patches

    def by_frame(part):
        wide = got[:, part * per_peer : (part + 1) * per_peer, :].astype(f32)
        wide = wide.reshape(peers, frames, patches, width)
        return [wide[:, f].reshape(count, width).astype(bf16) for f in range(frames)]

    low, high, heads = by_frame(0), by_frame(1), by_frame(2)
    for f in range(frames):
        grad[f, :, :width] = low[f]
        grad[f, :, width:] = high[f]
    results = fetch([(grad, grad_ref)], sems)
    for f in range(frames):
        projected = mm(heads[f][:, :HALF], w_mine[...], NT) + mm(heads[f][:, HALF:], w_other[...], NT)
        result[f] = (x[f].astype(f32) + projected).astype(bf16)
    wait_all(results + fetch([(result, result_ref)], sems, 1))


def vmem_params(mib=60):
    return pltpu.CompilerParams(vmem_limit_bytes=mib * 2**20)


def exchange(value):
    return lax.ppermute(value, "core", [(0, 1), (1, 0)])


def swap(value, axes):
    return lax.all_to_all(value, axes, split_axis=0, concat_axis=0, tiled=True)


def along_y(value, step):
    return lax.ppermute(value, "y", [(i, (i + step) % Y_SIZE) for i in range(Y_SIZE)])


def across_x(value):
    return lax.ppermute(value, "xh", [(0, 1), (1, 0)])


def body(frames_in, gain, w_qkv, w_out, out_grad):
    _, frames, patch_count, width = frames_in.shape
    tm = TM_SIZE
    patches = patch_count // tm
    per_peer = frames * patches
    rows = tm * per_peer
    shard = w_qkv.shape[0]
    core = lax.axis_index("core")
    first = core == 0
    gain_row = gain.reshape(1, width)

    def by_patch(value):
        value = value.reshape(frames, tm, patches, width).transpose(1, 0, 2, 3)
        return value.reshape(tm, per_peer, width)

    w_parts = pl.pallas_call(
        pack_weights_kernel,
        out_shape=jax.ShapeDtypeStruct((tm, 2 * shard, width), bf16),
        in_specs=[VMEM] * 2,
        compiler_params=vmem_params(),
        cost_estimate=pl.CostEstimate(flops=0, bytes_accessed=2**18, transcendentals=0),
        name="pack_weights",
    )(w_qkv, w_out.T)
    w_got = swap(w_parts.reshape(-1, width), TM).reshape(tm, 2, shard, width)

    sent = jnp.concatenate([by_patch(frames_in), by_patch(out_grad)], axis=1)
    sent, w_got = lax.optimization_barrier((sent, w_got))

    w_keep = lax.dynamic_index_in_dim(w_got, core, 1, keepdims=False).reshape(tm * shard, width)
    w_send = lax.dynamic_index_in_dim(w_got, 1 - core, 1, keepdims=False).reshape(tm * shard, width)
    w_recv = exchange(w_send)
    w_block = jnp.concatenate(
        [jnp.where(first, w_keep, w_recv), jnp.where(first, w_recv, w_keep)], axis=0
    )
    block = w_block.shape[0]

    got = swap(sent.reshape(-1, width), TM).reshape(tm, 2 * per_peer, width)

    pieces = []
    for part in (w_block, across_x(w_block)):
        pieces += [part] + [along_y(part, step) for step in range(1, Y_SIZE)]
    got_other = exchange(got)

    shape = jax.ShapeDtypeStruct
    token = pl.pallas_call(
        arrived_kernel,
        in_specs=[ANY] * 8,
        out_specs=VMEM,
        out_shape=shape((8, 128), f32),
        compiler_params=vmem_params(),
        cost_estimate=pl.CostEstimate(flops=2 * 10**10, bytes_accessed=4 * 2**20, transcendentals=0),
        name="arrived",
    )(*pieces)

    sample_shapes = (shape((rows, width + HALF), f32), shape((rows, width + HALF), bf16))
    half_shape, own_shape = shape((block, width), bf16), shape((block, width), f32)
    w_mine, for_own, for_other, *grad_pieces = pl.pallas_call(
        functools.partial(layer_kernel, patches),
        in_specs=[ANY, ANY, VMEM, VMEM] + [ANY] * 8,
        out_specs=(ANY,) * 11,
        out_shape=(shape((width, HALF), bf16),)
        + sample_shapes + ((own_shape,) + (half_shape,) * (Y_SIZE - 1)) * 2,
        scratch_shapes=[
            pltpu.VMEM((2,) + got.shape, bf16),
            pltpu.VMEM((width, width), bf16),
            pltpu.VMEM((2, rows, width), bf16),
            pltpu.VMEM((2, rows, HALF), bf16),
            pltpu.VMEM((2, rows, 3 * HALF), bf16),
            pltpu.VMEM((rows, width + HALF), f32),
            pltpu.VMEM((rows, width + HALF), bf16),
            pltpu.VMEM((width, width), f32),
            pltpu.VMEM((2, block, width), f32),
            pltpu.VMEM((6, block, width), bf16),
            pltpu.VMEM((HALF // DH, rows, rows), f32),
            pltpu.VMEM((HALF // DH, rows, rows), f32),
            pltpu.VMEM((HALF // DH, rows, rows), bf16),
            pltpu.VMEM((HALF // DH, rows, rows), bf16),
            pltpu.SemaphoreType.DMA((10,)),
            pltpu.SemaphoreType.DMA((11,)),
        ],
        compiler_params=vmem_params(60),
        cost_estimate=pl.CostEstimate(flops=3 * 10**10, bytes_accessed=10 * 2**20, transcendentals=2**19),
        name="layer",
    )(got, got_other, gain_row, token, *pieces)
    w_other = exchange(w_mine)
    from_other = exchange(for_other)

    received = [along_y(grad_pieces[Y_SIZE + step], step) for step in range(1, Y_SIZE)]
    partial = grad_pieces[Y_SIZE] + sum(piece.astype(f32) for piece in received)
    received = [along_y(grad_pieces[step], step) for step in range(1, Y_SIZE)]
    grads = pl.pallas_call(
        sum_kernel,
        in_specs=[VMEM] * 5,
        out_shape=shape((tm, 2 * shard, width), bf16),
        compiler_params=vmem_params(8),
        cost_estimate=pl.CostEstimate(flops=10**10, bytes_accessed=2 * 2**20, transcendentals=0),
        name="sum_blocks",
    )(grad_pieces[0], *received, across_x(partial.astype(bf16)))

    sent = pl.pallas_call(
        input_kernel,
        out_shape=shape((tm, 3 * per_peer, width // 2), bf16),
        in_specs=[ANY] * 2 + [VMEM] * 2,
        out_specs=ANY,
        scratch_shapes=[
            pltpu.VMEM(got.shape, bf16),
            pltpu.VMEM((rows, width + HALF), f32),
            pltpu.VMEM((tm, 3 * per_peer, width // 2), bf16),
            pltpu.SemaphoreType.DMA((6,)),
        ],
        compiler_params=vmem_params(24),
        cost_estimate=pl.CostEstimate(flops=10**9, bytes_accessed=6 * 2**20, transcendentals=0),
        name="input_gradient",
    )(got, for_own, from_other, gain_row)
    got = swap(sent.reshape(-1, width // 2), TM).reshape(sent.shape)
    grads, got = lax.optimization_barrier((grads, got))
    local = shape(frames_in.shape[1:], bf16)
    result, grad_in = pl.pallas_call(
        home_kernel,
        in_specs=[ANY] * 4,
        out_specs=(ANY,) * 2,
        out_shape=(local,) * 2,
        scratch_shapes=[
            pltpu.VMEM(sent.shape, bf16),
            pltpu.VMEM(local.shape, bf16),
            pltpu.VMEM((width, HALF), bf16),
            pltpu.VMEM((width, HALF), bf16),
            pltpu.VMEM(local.shape, bf16),
            pltpu.VMEM(local.shape, bf16),
            pltpu.SemaphoreType.DMA((4,)),
        ],
        compiler_params=vmem_params(),
        cost_estimate=pl.CostEstimate(flops=3 * 10**8, bytes_accessed=4 * 2**20, transcendentals=0),
        name="home",
    )(got, frames_in[0], w_mine, w_other)

    grads = swap(grads.reshape(-1, width), TM)
    grads, result, grad_in = lax.optimization_barrier((grads, result, grad_in))
    total = jnp.sum(grads.reshape(tm, 2, shard, width).astype(f32), axis=0)
    keep = lax.dynamic_index_in_dim(total, core, 0, keepdims=False)
    recv = exchange(lax.dynamic_index_in_dim(total, 1 - core, 0, keepdims=False))
    low = jnp.where(first, keep, recv).reshape(shard, 4, 1, HALF)
    high = jnp.where(first, recv, keep).reshape(shard, 4, 1, HALF)
    whole = jnp.concatenate([low, high], axis=2)
    grad_qkv = whole[:, :3].reshape(shard, 6 * HALF)
    grad_out = whole[:, 3].reshape(shard, 2 * HALF).T
    own_row = lax.axis_index(DP + TM) * shard
    grad_gain = jnp.sum(w_qkv.astype(f32) * grad_qkv, axis=1) / lax.dynamic_slice_in_dim(gain, own_row, shard)
    return (result[None], grad_in[None], grad_qkv, grad_out, grad_gain)


def solution(mesh):
    fine = Mesh(mesh.devices.reshape(Y_SIZE, XH_SIZE, 2, 2, 8), DP + TM)
    in_specs = (
        P(DP, TM, None, None),
        P(),
        P(DP + TM, None),
        P(None, DP + TM),
        P(DP, TM, None, None),
    )
    out_specs = (
        P(DP, TM, None, None),
        P(DP, TM, None, None),
        P(DP + TM, None),
        P(None, DP + TM),
        P(DP + TM),
    )
    return jax.shard_map(body, mesh=fine, in_specs=in_specs, out_specs=out_specs, check_vma=False)
```

```python
import functools

import jax
import jax.numpy as jnp
from jax import lax
from jax.experimental import pallas as pl
from jax.experimental.pallas import tpu as pltpu
from jax.sharding import Mesh, PartitionSpec as P

DP = ("y", "xh", "core")
TM = ("xl", "z")
Y_SIZE, XH_SIZE, TM_SIZE = 4, 2, 16

D = 1024
DH = 64
HALF = 256
norm_eps = 1e-05
f32 = jnp.float32
bf16 = jnp.bfloat16

NN = (((1,), (0,)), ((), ()))
NT = (((1,), (1,)), ((), ()))
TN = (((0,), (0,)), ((), ()))

VMEM = pl.BlockSpec(memory_space=pltpu.VMEM)
ANY = pl.BlockSpec(memory_space=pl.ANY)


def mm(a, b, dims):
    return lax.dot_general(a, b, dims, preferred_element_type=f32)


def layer_stats(features):
    wide = features.astype(f32)
    centred = wide - jnp.mean(wide, axis=-1, keepdims=True)
    inv_std = lax.rsqrt(jnp.mean(centred * centred, axis=-1, keepdims=True) + norm_eps)
    return centred * inv_std, inv_std


def pack_weights_kernel(w_qkv_ref, w_out_ref, out_ref):
    qkv, out = w_qkv_ref[...].astype(f32), w_out_ref[...].astype(f32)
    halves = []
    for half in range(2):
        parts = [qkv[:, (2 * part + half) * HALF : (2 * part + half + 1) * HALF] for part in range(3)]
        halves.append(jnp.concatenate(parts + [out[:, half * HALF : (half + 1) * HALF]], axis=1))
    both = jnp.concatenate(halves, axis=0)
    out_ref[...] = jnp.broadcast_to(both[None], out_ref.shape).astype(bf16)


def fetch(pairs, sems, first=0):
    copies = [pltpu.make_async_copy(src, dst, sems.at[first + i]) for i, (src, dst) in enumerate(pairs)]
    for copy in copies:
        copy.start()
    return copies


def wait_all(copies):
    for copy in copies:
        copy.wait()


CHUNK = 64


def sample(patches, got, gain_ref, weights, normed, mixed, dpacked, slots, before_weights):
    scores, d_probs, low_probs, d_scores = slots
    rows = normed.shape[0]
    per_peer = got.shape[1] // 2
    group = 4
    for peer in range(0, got.shape[0], group):
        features = got[peer : peer + group, :per_peer, :].reshape(group * per_peer, D)
        normal_x, _ = layer_stats(features)
        normed[peer * per_peer : (peer + group) * per_peer, :] = (normal_x * gain_ref[...]).astype(bf16)
    before_weights()
    packed = mm(normed[...], weights[:, : 3 * HALF], NN).astype(bf16)
    d_mixed = mm(got[:, per_peer:, :].reshape(rows, D), weights[:, 3 * HALF :], NN).astype(bf16)
    row_patch = lax.broadcasted_iota(jnp.int32, (CHUNK, rows), 0) % patches
    col_patch = lax.broadcasted_iota(jnp.int32, (CHUNK, rows), 1) % patches
    bias = jnp.where(row_patch == col_patch, 0.0, -1e30)
    low_half = lax.broadcasted_iota(jnp.int32, (rows, 2 * DH), 1) < DH
    zero = jnp.zeros((rows, 2 * DH), bf16)
    heads = HALF // DH

    def part(index, head):
        lo = index * HALF + head // 2 * 2 * DH
        return packed[:, lo : lo + 2 * DH]

    def d_part(head):
        lo = head // 2 * 2 * DH
        return d_mixed[:, lo : lo + 2 * DH]

    for head in range(heads):
        own = low_half if head % 2 == 0 else jnp.logical_not(low_half)
        query = jnp.where(own, part(0, head) * DH ** (-0.5), zero)
        scores[head] = mm(query, part(1, head), NT)
        d_probs[head] = mm(jnp.where(own, d_part(head), zero), part(2, head), NT)
    for pair in range(heads // 2):
        outs = []
        for head in (2 * pair, 2 * pair + 1):
            for at in range(0, rows, CHUNK):
                score = scores[head, at : at + CHUNK, :] + bias
                expo = jnp.exp(score - jnp.max(score, axis=-1, keepdims=True))
                prob = expo * (1.0 / jnp.sum(expo, axis=-1, keepdims=True))
                low_probs[head, at : at + CHUNK, :] = prob.astype(bf16)
                d_prob = d_probs[head, at : at + CHUNK, :]
                inner = jnp.sum(d_prob * prob, axis=-1, keepdims=True)
                d_scores[head, at : at + CHUNK, :] = (prob * (d_prob - inner)).astype(bf16)
            outs.append(
                (
                    mm(low_probs[head], part(2, head), NN),
                    mm(d_scores[head], part(1, head), NN) * DH ** (-0.5),
                    mm(d_scores[head], part(0, head), TN) * DH ** (-0.5),
                    mm(low_probs[head], d_part(head), TN),
                )
            )
        outs = [jnp.where(low_half, low, high).astype(bf16) for low, high in zip(*outs)]
        lo = pair * 2 * DH
        mixed[:, lo : lo + 2 * DH] = outs[0]
        for index in range(3):
            at = index * HALF + lo
            dpacked[:, at : at + 2 * DH] = outs[1 + index]


def block_of(step, side):
    y, xh = lax.axis_index("y"), lax.axis_index("xh")
    return lax.rem(y + step + Y_SIZE, Y_SIZE) * XH_SIZE + lax.rem(xh + side, XH_SIZE)


def arrived_kernel(*refs):
    refs[-1][...] = jnp.zeros_like(refs[-1])


def layer_kernel(patches, got_own_ref, got_other_ref, gain_ref, token_ref, *refs):
    pieces, outs, grad_refs, scratch = refs[:8], refs[8:11], refs[11:19], refs[19:]
    w_ref, for_own_ref, for_other_ref = outs
    got, weights, normed, mixed, dpacked, for_own, for_other, grads, own, peers = scratch[:10]
    slots, (sems, out_sems) = scratch[10:14], scratch[14:]
    copies = fetch([(got_own_ref, got.at[0])], sems)
    block = own.shape[1]
    places = [block_of(-(i % Y_SIZE), i // Y_SIZE) for i in range(8)]
    starts = [pl.multiple_of(place * block, block) for place in places]
    copies += fetch([(p, weights.at[pl.ds(at, block), :]) for p, at in zip(pieces, starts)], sems, 1)
    copies += fetch([(got_other_ref, got.at[1])], sems, 9)
    results = []
    per_peer = got.shape[2] // 2

    def before_weights():
        wait_all(copies[1:9])
        results.extend(fetch([(weights.at[:, 3 * HALF :], w_ref)], out_sems))

    copies[0].wait()
    arguments = (got.at[0], gain_ref, weights, normed.at[0], mixed.at[0], dpacked.at[0])
    sample(patches, *arguments, slots, before_weights)
    for_own[:, :D] = mm(dpacked[0], weights[:, : 3 * HALF], NT)
    for_own[:, D:] = mixed[0].astype(f32)
    results += fetch([(for_own, for_own_ref)], out_sems, 1)
    copies[9].wait()
    arguments = (got.at[1], gain_ref, weights, normed.at[1], mixed.at[1], dpacked.at[1])
    sample(patches, *arguments, slots, lambda: None)
    for_other[:, :D] = mm(dpacked[1], weights[:, : 3 * HALF], NT).astype(bf16)
    for_other[:, D:] = mixed[1]
    results += fetch([(for_other, for_other_ref)], out_sems, 2)
    rows = normed.shape[1]
    pair_rows = 2 * block
    all_dpacked = dpacked[...].reshape(2 * rows, 3 * HALF)
    all_mixed = mixed[...].reshape(2 * rows, HALF)
    for part in range(Y_SIZE):
        columns = slice(part * pair_rows, (part + 1) * pair_rows)
        grads[columns, : 3 * HALF] = mm(normed[:, :, columns].reshape(2 * rows, pair_rows), all_dpacked, TN)
        grads[columns, 3 * HALF :] = mm(got[:, :, per_peer:, columns].reshape(2 * rows, pair_rows), all_mixed, TN)
    for step in (1, 2, 3, 0):
        for side in range(XH_SIZE):
            start = pl.multiple_of(block_of(step, side) * block, block)
            slot = own.at[side] if step == 0 else peers.at[side * (Y_SIZE - 1) + step - 1]
            slot[...] = grads[pl.ds(start, block), :].astype(slot.dtype)
            results += fetch([(slot, grad_refs[side * Y_SIZE + step])], out_sems, len(results))
    wait_all(results)


def input_kernel(got_ref, mine_ref, other, gain_ref, out_ref, got, mine, out, sems):
    copies = fetch([(got_ref, got), (mine_ref, mine)], sems)
    peers, per_peer = got.shape[0], got.shape[1] // 2
    wait_all(copies)
    results = []
    group = 4
    half = (group, per_peer, D // 2)
    for peer in range(0, peers, group):
        at = slice(peer, peer + group)
        rows = slice(peer * per_peer, (peer + group) * per_peer)
        normal_x, inv_std = layer_stats(got[at, :per_peer, :].reshape(group * per_peer, D))
        scaled = (mine[rows, :D] + other[rows, :D].astype(f32)).astype(bf16).astype(f32) * gain_ref[...]
        d_input = inv_std * (
            scaled
            - jnp.mean(scaled, axis=-1, keepdims=True)
            - normal_x * jnp.mean(scaled * normal_x, axis=-1, keepdims=True)
        )
        grad_in = (got[at, per_peer:, :].reshape(group * per_peer, D).astype(f32) + d_input).astype(bf16)
        out[at, :per_peer, :] = grad_in[:, : D // 2].reshape(half)
        out[at, per_peer : 2 * per_peer, :] = grad_in[:, D // 2 :].reshape(half)
        out[at, 2 * per_peer :, :HALF] = mine[rows, D:].astype(bf16).reshape(group, per_peer, HALF)
        out[at, 2 * per_peer :, HALF:] = other[rows, D:].reshape(group, per_peer, HALF)
        results += fetch([(out.at[at], out_ref.at[at])], sems, 2 + len(results))
    wait_all(results)


def sum_kernel(own_ref, a_ref, b_ref, c_ref, across_ref, out_ref):
    total = own_ref[...] + a_ref[...].astype(f32) + b_ref[...].astype(f32) + c_ref[...].astype(f32)
    total = total + across_ref[...].astype(f32)
    shard = 4
    low, high = (total.reshape(2, -1, 2 * shard, D)[core] for core in range(2))
    top = lax.broadcasted_iota(jnp.int32, low.shape, 1) < shard
    even = jnp.where(top, low, pltpu.roll(high, shard, 1))
    odd = jnp.where(top, pltpu.roll(low, shard, 1), high)
    out_ref[...] = jnp.stack([even, odd], axis=1).reshape(out_ref.shape).astype(bf16)


def home_kernel(got_ref, x_ref, w_mine_ref, w_other_ref, result_ref, grad_ref, got, x, w_mine, w_other, result, grad, sems):
    wait_all(
        fetch(
            [(got_ref, got), (x_ref, x), (w_mine_ref, w_mine), (w_other_ref, w_other)],
            sems,
        )
    )
    peers, _, width = got.shape
    frames, count, _ = x.shape
    patches = count // peers
    per_peer = frames * patches

    def by_frame(part):
        wide = got[:, part * per_peer : (part + 1) * per_peer, :].astype(f32)
        wide = wide.reshape(peers, frames, patches, width)
        return [wide[:, f].reshape(count, width).astype(bf16) for f in range(frames)]

    low, high, heads = by_frame(0), by_frame(1), by_frame(2)
    for f in range(frames):
        grad[f, :, :width] = low[f]
        grad[f, :, width:] = high[f]
    results = fetch([(grad, grad_ref)], sems)
    for f in range(frames):
        projected = mm(heads[f][:, :HALF], w_mine[...], NT) + mm(heads[f][:, HALF:], w_other[...], NT)
        result[f] = (x[f].astype(f32) + projected).astype(bf16)
    wait_all(results + fetch([(result, result_ref)], sems, 1))


def vmem_params(mib=60):
    return pltpu.CompilerParams(vmem_limit_bytes=mib * 2**20)


def exchange(value):
    return lax.ppermute(value, "core", [(0, 1), (1, 0)])


def swap(value, axes):
    return lax.all_to_all(value, axes, split_axis=0, concat_axis=0, tiled=True)


def along_y(value, step):
    return lax.ppermute(value, "y", [(i, (i + step) % Y_SIZE) for i in range(Y_SIZE)])


def across_x(value):
    return lax.ppermute(value, "xh", [(0, 1), (1, 0)])


def body(frames_in, gain, w_qkv, w_out, out_grad):
    _, frames, patch_count, width = frames_in.shape
    tm = TM_SIZE
    patches = patch_count // tm
    per_peer = frames * patches
    rows = tm * per_peer
    shard = w_qkv.shape[0]
    core = lax.axis_index("core")
    first = core == 0
    gain_row = gain.reshape(1, width)

    def by_patch(value):
        value = value.reshape(frames, tm, patches, width).transpose(1, 0, 2, 3)
        return value.reshape(tm, per_peer, width)

    w_parts = pl.pallas_call(
        pack_weights_kernel,
        out_shape=jax.ShapeDtypeStruct((tm, 2 * shard, width), bf16),
        in_specs=[VMEM] * 2,
        compiler_params=vmem_params(),
        cost_estimate=pl.CostEstimate(flops=0, bytes_accessed=2**18, transcendentals=0),
        name="pack_weights",
    )(w_qkv, w_out.T)
    w_got = swap(w_parts.reshape(-1, width), TM).reshape(tm, 2, shard, width)

    sent = jnp.concatenate([by_patch(frames_in), by_patch(out_grad)], axis=1)
    own_row = lax.axis_index(DP + TM) * shard
    gain_inverse = 1.0 / lax.dynamic_slice_in_dim(gain, own_row, shard)
    sent, w_got, gain_inverse = lax.optimization_barrier((sent, w_got, gain_inverse))

    w_keep = lax.dynamic_index_in_dim(w_got, core, 1, keepdims=False).reshape(tm * shard, width)
    w_send = lax.dynamic_index_in_dim(w_got, 1 - core, 1, keepdims=False).reshape(tm * shard, width)
    w_recv = exchange(w_send)
    w_block = jnp.concatenate(
        [jnp.where(first, w_keep, w_recv), jnp.where(first, w_recv, w_keep)], axis=0
    )
    block = w_block.shape[0]

    got = swap(sent.reshape(-1, width), TM).reshape(tm, 2 * per_peer, width)

    pieces = []
    for part in (w_block, across_x(w_block)):
        pieces += [part] + [along_y(part, step) for step in range(1, Y_SIZE)]
    got_other = exchange(got)

    shape = jax.ShapeDtypeStruct
    token = pl.pallas_call(
        arrived_kernel,
        in_specs=[ANY] * 8,
        out_specs=VMEM,
        out_shape=shape((8, 128), f32),
        compiler_params=vmem_params(),
        cost_estimate=pl.CostEstimate(flops=2 * 10**10, bytes_accessed=4 * 2**20, transcendentals=0),
        name="arrived",
    )(*pieces)

    sample_shapes = (shape((rows, width + HALF), f32), shape((rows, width + HALF), bf16))
    half_shape, own_shape = shape((block, width), bf16), shape((block, width), f32)
    w_mine, for_own, for_other, *grad_pieces = pl.pallas_call(
        functools.partial(layer_kernel, patches),
        in_specs=[ANY, ANY, VMEM, VMEM] + [ANY] * 8,
        out_specs=(ANY,) * 11,
        out_shape=(shape((width, HALF), bf16),)
        + sample_shapes + ((own_shape,) + (half_shape,) * (Y_SIZE - 1)) * 2,
        scratch_shapes=[
            pltpu.VMEM((2,) + got.shape, bf16),
            pltpu.VMEM((width, width), bf16),
            pltpu.VMEM((2, rows, width), bf16),
            pltpu.VMEM((2, rows, HALF), bf16),
            pltpu.VMEM((2, rows, 3 * HALF), bf16),
            pltpu.VMEM((rows, width + HALF), f32),
            pltpu.VMEM((rows, width + HALF), bf16),
            pltpu.VMEM((width, width), f32),
            pltpu.VMEM((2, block, width), f32),
            pltpu.VMEM((6, block, width), bf16),
            pltpu.VMEM((HALF // DH, rows, rows), f32),
            pltpu.VMEM((HALF // DH, rows, rows), f32),
            pltpu.VMEM((HALF // DH, rows, rows), bf16),
            pltpu.VMEM((HALF // DH, rows, rows), bf16),
            pltpu.SemaphoreType.DMA((10,)),
            pltpu.SemaphoreType.DMA((11,)),
        ],
        compiler_params=vmem_params(60),
        cost_estimate=pl.CostEstimate(flops=3 * 10**10, bytes_accessed=10 * 2**20, transcendentals=2**19),
        name="layer",
    )(got, got_other, gain_row, token, *pieces)
    w_other = exchange(w_mine)
    from_other = exchange(for_other)

    received = [along_y(grad_pieces[Y_SIZE + step], step) for step in range(1, Y_SIZE)]
    partial = grad_pieces[Y_SIZE] + sum(piece.astype(f32) for piece in received)
    received = [along_y(grad_pieces[step], step) for step in range(1, Y_SIZE)]
    grads = pl.pallas_call(
        sum_kernel,
        in_specs=[VMEM] * 5,
        out_shape=shape((tm, 2 * shard, width), bf16),
        compiler_params=vmem_params(8),
        cost_estimate=pl.CostEstimate(flops=10**10, bytes_accessed=2 * 2**20, transcendentals=0),
        name="sum_blocks",
    )(grad_pieces[0], *received, across_x(partial.astype(bf16)))

    sent = pl.pallas_call(
        input_kernel,
        out_shape=shape((tm, 3 * per_peer, width // 2), bf16),
        in_specs=[ANY] * 2 + [VMEM] * 2,
        out_specs=ANY,
        scratch_shapes=[
            pltpu.VMEM(got.shape, bf16),
            pltpu.VMEM((rows, width + HALF), f32),
            pltpu.VMEM((tm, 3 * per_peer, width // 2), bf16),
            pltpu.SemaphoreType.DMA((6,)),
        ],
        compiler_params=vmem_params(24),
        cost_estimate=pl.CostEstimate(flops=10**9, bytes_accessed=6 * 2**20, transcendentals=0),
        name="input_gradient",
    )(got, for_own, from_other, gain_row)
    got = swap(sent.reshape(-1, width // 2), TM).reshape(sent.shape)
    grads, got = lax.optimization_barrier((grads, got))
    local = shape(frames_in.shape[1:], bf16)
    result, grad_in = pl.pallas_call(
        home_kernel,
        in_specs=[ANY] * 4,
        out_specs=(ANY,) * 2,
        out_shape=(local,) * 2,
        scratch_shapes=[
            pltpu.VMEM(sent.shape, bf16),
            pltpu.VMEM(local.shape, bf16),
            pltpu.VMEM((width, HALF), bf16),
            pltpu.VMEM((width, HALF), bf16),
            pltpu.VMEM(local.shape, bf16),
            pltpu.VMEM(local.shape, bf16),
            pltpu.SemaphoreType.DMA((4,)),
        ],
        compiler_params=vmem_params(),
        cost_estimate=pl.CostEstimate(flops=3 * 10**8, bytes_accessed=4 * 2**20, transcendentals=0),
        name="home",
    )(got, frames_in[0], w_mine, w_other)

    grads = swap(grads.reshape(-1, width), TM)
    grads, result, grad_in = lax.optimization_barrier((grads, result, grad_in))
    total = jnp.sum(grads.reshape(tm, 2, shard, width).astype(f32), axis=0)
    keep = lax.dynamic_index_in_dim(total, core, 0, keepdims=False)
    recv = exchange(lax.dynamic_index_in_dim(total, 1 - core, 0, keepdims=False))
    low, high = jnp.where(first, keep, recv), jnp.where(first, recv, keep)
    whole = [half[:, part * HALF : (part + 1) * HALF] for part in range(4) for half in (low, high)]
    grad_qkv = jnp.concatenate(whole[:6], axis=1)
    grad_out = jnp.concatenate(whole[6:], axis=1).T
    grad_gain = jnp.sum(w_qkv.astype(f32) * grad_qkv * gain_inverse[:, None], axis=1)
    return (result[None], grad_in[None], grad_qkv, grad_out, grad_gain)


def solution(mesh):
    fine = Mesh(mesh.devices.reshape(Y_SIZE, XH_SIZE, 2, 2, 8), DP + TM)
    in_specs = (
        P(DP, TM, None, None),
        P(),
        P(DP + TM, None),
        P(None, DP + TM),
        P(DP, TM, None, None),
    )
    out_specs = (
        P(DP, TM, None, None),
        P(DP, TM, None, None),
        P(DP + TM, None),
        P(None, DP + TM),
        P(DP + TM),
    )
    return jax.shard_map(body, mesh=fine, in_specs=in_specs, out_specs=out_specs, check_vma=False)
```
